128 devices in a mesh: front: 16 (over x, z), grp: 8 (over y, core).
Axes of the slice: x: 4, y: 4, z: 4, core: 2. Of those that a mesh axis runs over, the one named last changes fastest.
Arguments:
- front_block: float32 [16, 16384, 1408], P('front', 'grp'), as said below
- child_blocks: float32 [16, 8, 4, 16, 1408], P('front', 'grp'), may hold values from -0.5 to 0.5
- child_rows: int32 [16, 8, 4, 16], P('front', 'grp'), may hold values from 0 to 2047
- child_dest: int32 [16, 8, 4, 1], P('front', 'grp'), may hold values from 0 to 15; in each aligned block of 4 rows (0 to 3, 4 to 7, ..., all dimensions but the last counted through in order) at most 2 rows name the same one
- panel_owner: int32 [16], P('front'), may hold values from 0 to 7
Outputs:
- panel_factor: float32 [16, 16384, 512], P('front', 'grp')
- schur_block: float32 [16, 16384, 896], P('front', 'grp')
The draws below stay inside these ranges and needn't reach their ends.
Inputs may be any that keep to these rules, and one draw needn't show every extreme that they name: `child_dest`: among the 4 blocks of one device no front is named more than 2 times, and in every draw some device names some front exactly 2 times. `front_block`: for every front and row block, the first 512 rows' leading 512 x 512 block has a positive diagonal that dominates; other entries lie within -2.3 to 2.3.
All inputs are finite; a program needn't handle non-finite values.
Results may differ from the reference program's by a relative error of at most 0.0003.
Values sent between devices are 32-bit elements; how exact they have to be, the bound alone decides.
A program may use at most 128 MiB of HBM per device.

```python
import math
import jax
import jax.numpy as jnp
import numpy as np
from jax import lax

NF = 16384
PB = 512
WIN = 896
KB = 4
BR = 16
CAP = 2
FRONTS = 16
GROUPS = 8
ROWS_DEV = 2048
COLS = 1408


def draw_front_block(key, part):
    key_base = jax.random.fold_in(key, 11)
    key_diag = jax.random.fold_in(key, 23)
    shape = (FRONTS, NF, COLS)
    entries = jax.random.uniform(key_base, shape, jnp.float32, -1.0, 1.0)
    local_row = jnp.arange(NF, dtype=jnp.int32) % ROWS_DEV
    column = jnp.arange(COLS, dtype=jnp.int32)
    is_diag = (local_row[:, None] == column[None, :]) & (local_row[:, None] < PB)
    boost = jax.random.uniform(key_diag, (FRONTS, NF, 1), jnp.float32, 2.0, 3.0) * jnp.sqrt(jnp.float32(PB))
    return entries + jnp.where(is_diag[None, :, :], boost, 0.0)


def touch_ends(array, stream_key, least, largest):
    shape = array.shape
    place = [jax.random.randint(jax.random.fold_in(stream_key, axis), (), 0, shape[axis]) for axis in range(len(shape))]
    array = array.at[tuple(place)].set(least)
    longest = shape.index(max(shape))
    place[longest] = (place[longest] + 1) % shape[longest]
    return array.at[tuple(place)].set(largest)


def steps_of(own_key, extent, pieces, low, largest):
    level = 1.0
    for axis_at, parts in pieces:
        heights = jax.random.uniform(jax.random.fold_in(jax.random.fold_in(own_key, 6), axis_at), (parts,), jnp.float32, low / len(pieces), largest / len(pieces))
        level = level * jnp.repeat(jnp.exp(heights), extent[axis_at] // parts).reshape((-1,) + (1,) * (len(extent) - 1 - axis_at))
    return level


def routed_block(key, own, number, rows, number_of, top, limit, skew):
    sequence = jax.random.permutation(key, number_of)
    packed, ordinary = load_shares(number_of, rows * top, limit, skew, True), load_shares(number_of, rows * top, limit, skew, False)
    places = jnp.arange(number_of)

    def named(lengths, rotation):
        used = int((lengths > 0).sum())
        fixed = max(1, used // 4)
        passed = fixed + (places - fixed + rotation * (used - fixed)) % max(1, number_of - fixed)
        return jnp.zeros((number_of,), jnp.int32).at[sequence[jnp.where(places < fixed, places, passed)]].set(jnp.asarray(lengths, jnp.int32))

    lengths = jnp.where(number % 4 == 0, named(packed, number // 4), named(ordinary, number - number // 4 - 1))
    mixed = jax.random.permutation(jax.random.fold_in(own, 3), number_of)
    giver, taker = mixed[0:number_of // 2 * 2:2], mixed[1:number_of // 2 * 2:2]
    slack = jnp.minimum(lengths[giver] - 1, limit - lengths[taker]) // 2
    slack = jnp.where((giver == sequence[0]) | (taker == sequence[0]) | (lengths[taker] == 0), 0, jnp.maximum(slack, 0))
    passed = jax.random.randint(jax.random.fold_in(own, 4), (number_of // 2,), 0, 1 << 20) % (slack + 1)
    lengths = lengths.at[giver].add(-passed).at[taker].add(passed)
    items = jnp.searchsorted(jnp.cumsum(lengths), jnp.arange(rows * top), side="right").astype(jnp.int32)
    grid = items.reshape(top, rows).T
    grid = grid[jax.random.permutation(jax.random.fold_in(own, 1), rows)]
    rotation = jax.random.randint(jax.random.fold_in(own, 2), (rows, 1), 0, top)
    return jnp.take_along_axis(grid, (jnp.arange(top)[None, :] + rotation) % top, axis=1)


def load_shares(number_of, total, limit, skew, full):
    loads = [(1 << 20) // math.isqrt(grade ** skew) + 1 for grade in range(1, number_of + 1)]
    largest = limit if full else min(limit, max(-(-total // number_of), total * loads[0] // sum(loads)))
    least = 1 if total - largest >= number_of - 1 else 0
    holding, rest = [largest] + [least] * (number_of - 1), total - largest - least * (number_of - 1)
    while rest > 0:
        movable = [i for i in range(1, number_of) if holding[i] < largest] or [i for i in range(1, number_of) if holding[i] < limit]
        whole, remaining = sum([loads[i] for i in movable]), rest
        for i in movable:
            addition = min(limit - holding[i], max(1, remaining * loads[i] // whole), rest)
            holding[i] = holding[i] + addition
            rest = rest - addition
    return np.array(holding)


def setup_inputs(seed: int = 0) -> dict:
    splits = jax.random.split(jax.random.key(seed), 6)
    front_block = draw_front_block(jax.random.fold_in(splits[5], 71), 0)
    child_blocks = jnp.clip(jax.random.uniform(splits[1], (FRONTS, GROUPS, KB, BR, COLS), jnp.float32, -0.5, 0.5) * steps_of(splits[1], (FRONTS, GROUPS, KB, BR, COLS), ((0, 16), (1, 8)), -0.4, 0.0), -0.5, 0.5)
    child_rows = touch_ends(jax.random.randint(splits[2], (FRONTS, GROUPS, KB, BR), 0, ROWS_DEV), jax.random.fold_in(splits[2], 1), 0, ROWS_DEV - 1).astype(jnp.int32)
    child_dest_keys = jax.random.split(jax.random.fold_in(splits[3], 1), FRONTS * GROUPS * KB // KB)
    child_dest_turns = jax.random.permutation(jax.random.fold_in(splits[3], 3), FRONTS * GROUPS * KB // KB)
    child_dest = jax.vmap(lambda own, number: routed_block(jax.random.fold_in(splits[3], 2), own, number, KB, FRONTS, 1, CAP, 2))(child_dest_keys, child_dest_turns).reshape((FRONTS, GROUPS, KB, 1))
    panel_owner = touch_ends(jax.random.randint(splits[4], (FRONTS,), 0, GROUPS), jax.random.fold_in(splits[4], 1), 0, GROUPS - 1).astype(jnp.int32)
    return {"front_block": front_block, "child_blocks": child_blocks, "child_rows": child_rows, "child_dest": child_dest, "panel_owner": panel_owner}


def right_solve(factor, rows):
    return lax.linalg.triangular_solve(factor, rows, left_side=False, lower=True, transpose_a=True)

def factor_front(pair):
    matrix, owner_index = pair
    start_row = (owner_index * ROWS_DEV).astype(jnp.int32)
    zero_index = jnp.zeros((), jnp.int32)
    pivot_block = lax.dynamic_slice(matrix, (start_row, zero_index), (PB, PB))
    symmetric = 0.5 * (pivot_block + pivot_block.T)
    pivot_factor = jnp.linalg.cholesky(symmetric)
    solved = right_solve(pivot_factor, matrix[:, :PB])
    window = lax.dynamic_slice(solved, (start_row + PB, zero_index), (WIN, PB))
    schur_part = matrix[:, PB:] - jnp.dot(solved, window.T, precision=lax.Precision.HIGHEST)
    panel_rows = lax.dynamic_update_slice(solved, pivot_factor, (start_row, zero_index))
    return (panel_rows, schur_part)

def reference(front_block, child_blocks, child_rows, child_dest, panel_owner):
    flattened = front_block.reshape(FRONTS * NF, COLS)
    group_base = (jnp.arange(GROUPS, dtype=jnp.int32) * ROWS_DEV)[None, :, None, None]
    target = child_dest[..., 0][..., None] * NF + group_base + child_rows
    flattened = flattened.at[target.reshape(-1)].add(child_blocks.reshape(-1, COLS))
    assembled = flattened.reshape(FRONTS, NF, COLS)
    panel_factor, schur_block = lax.map(factor_front, (assembled, panel_owner))
    return (panel_factor, schur_block)
```

```python
import functools

import jax
import jax.numpy as jnp
from jax import lax
from jax.experimental import pallas as pl
from jax.experimental.pallas import tpu as pltpu
from jax.sharding import PartitionSpec as P

F32, BF16 = jnp.float32, jnp.bfloat16
MESH = pl.DeviceIdType.MESH
PB, WIN, KB, BR, CAP = 512, 896, 4, 16, 2
NFRONT, NCHIP = 16, 4
SLOT = CAP * BR
KALL = NFRONT * SLOT
NB = 128
STEPS = PB // NB
SB = 16
CHUNKS = 7
PIECE = WIN // (4 * CHUNKS)
TURNS = CHUNKS + 3

NN = (((1,), (0,)), ((), ()))
NT = (((1,), (1,)), ((), ()))
TN = (((0,), (0,)), ((), ()))


def split(x):
    high = x.astype(BF16).astype(F32)
    return high, x - high


def dot(a, b, dims):
    return lax.dot_general(a.astype(BF16), b.astype(BF16), dims, preferred_element_type=F32)


def dot3(a, b, dims):
    ah, al = split(a)
    bh, bl = split(b)
    return dot(ah, bh, dims) + (dot(ah, bl, dims) + dot(al, bh, dims))


def eliminate(d_ref, k):
    n, b, c0 = NB, SB, k * SB
    lane = lax.broadcasted_iota(jnp.int32, (1, n), 1)
    rows = [d_ref[pl.ds(c0 + i, 1), :] for i in range(b)]
    s = [[None] * b for _ in range(b)]
    for j in range(b):
        for i in range(j, b):
            s[i][j] = jnp.broadcast_to(rows[j][:, c0 + i : c0 + i + 1], (1, n))
    inside = (lane >= c0) & (lane < c0 + b)
    rows = [jnp.where(inside, jnp.where(lane == c0 + i, 1.0, 0.0), rows[i]) for i in range(b)]
    for j in range(b):
        inv = lax.rsqrt(s[j][j])
        for i in range(j + 1, b):
            s[i][j] = s[i][j] * inv
        rows[j] = rows[j] * inv
        for i in range(j + 1, b):
            for q in range(j + 1, i + 1):
                s[i][q] = s[i][q] - s[i][j] * s[q][j]
        for i in range(j + 1, b):
            rows[i] = rows[i] - s[i][j] * rows[j]
        d_ref[pl.ds(c0 + j, 1), :] = rows[j]
    if c0 + b < n:
        u = d_ref[pl.ds(c0, b), :]
        col = lax.broadcasted_iota(jnp.int32, (b, n), 1)
        left = jnp.where(col >= c0 + b, u, 0.0)
        uh, ul = split(u)
        lh, ll = split(left)
        update = dot(jnp.concatenate([lh, lh, ll], 0), jnp.concatenate([uh, ul, uh], 0), TN)
        below = n - c0 - b
        old = d_ref[pl.ds(c0 + b, below), :]
        col = lax.broadcasted_iota(jnp.int32, (below, n), 1)
        old = jnp.where((col >= c0) & (col < c0 + b), 0.0, old)
        d_ref[pl.ds(c0 + b, below), :] = old - update[c0 + b :, :]


def gather_kernel(
    front_ref, blocks_ref, rows_ref, dest_ref, owner_ref,
    win_out, w_out, sym_out, panel_out, trail_out, index_out,
    part, rowbuf, send_p, send_t, send_i, got_p, got_t, got_i,
    table, diag, pre_win, ring_in, ring_out, pair_in,
    pre_w, chip_w, far_w, half_w, pair_w,
    load_sem, own_sem, xs_sem, xr_sem, pw_sem, rs_sem, rr_sem, ps_sem, pr_sem,
    qs_sem, qr_sem, fs_sem, fr_sem, hs_sem, hr_sem,
):
    front = lax.axis_index("front")
    group = lax.axis_index("grp")
    chip, core = group // 2, group % 2
    rest = PB + WIN

    load = pltpu.make_async_copy(front_ref.at[0, pl.ds(0, rest), pl.ds(0, PB)], part, load_sem)
    load.start()

    barrier = pltpu.get_barrier_semaphore()

    def greet(step, carry):
        pl.semaphore_signal(barrier, inc=1, device_id={"front": lax.rem(front + step, NFRONT)}, device_id_type=MESH)
        return carry

    lax.fori_loop(1, NFRONT, greet, 0)
    partner = 2 * chip + (1 - core)
    pl.semaphore_signal(barrier, inc=1, device_id={"grp": partner}, device_id_type=MESH)
    for step in range(1, NCHIP):
        there = 2 * lax.rem(chip + step, NCHIP) + core
        pl.semaphore_signal(barrier, inc=1, device_id={"grp": there}, device_id_type=MESH)

    rowbuf[...] = jnp.zeros_like(rowbuf)
    rowbuf[0:KB, 0:BR] = rows_ref[...]
    spread = rowbuf[...]
    for width in (16, 32, 64):
        spread = spread + pltpu.roll(spread, width, 1)
    rowbuf[...] = spread
    dests = [dest_ref[k] for k in range(KB)]
    ranks = []
    for k in range(KB):
        rank = jnp.int32(0)
        for e in range(k):
            rank = rank + (dests[e] == dests[k]).astype(jnp.int32)
        ranks.append(rank)
    lane = lax.broadcasted_iota(jnp.int32, (8, 128), 1)
    mine = lax.rem(front, 4) * SLOT

    def choose(to, slot):
        pick, found = jnp.int32(0), jnp.int32(0)
        for k in range(KB):
            hit = ((dests[k] == to) & (ranks[k] == slot)).astype(jnp.int32)
            pick = pick + hit * k
            found = found + hit
        return pick, found

    def pack_panel(to, carry):
        index = jnp.zeros((8, 128), jnp.int32)
        for slot in range(CAP):
            pick, found = choose(to, slot)
            send_p[to, slot * BR : (slot + 1) * BR, :] = blocks_ref[pick, :, 0:PB]
            at = jnp.broadcast_to(rowbuf[pl.ds(pick, 1), :], (8, 128))
            at = jnp.where(found > 0, at, -1)
            base = mine + slot * BR
            index = jnp.where((lane >= base) & (lane < base + BR), at, index)
        send_i[to] = index
        return carry

    lax.fori_loop(0, NFRONT, pack_panel, 0)
    pl.semaphore_wait(barrier, NFRONT - 1 + 1 + NCHIP - 1)

    def exchange(src, dst, kind, step):
        to = lax.rem(front + step, NFRONT)
        return pltpu.make_async_remote_copy(
            src_ref=src.at[to], dst_ref=dst.at[front],
            send_sem=xs_sem.at[kind, step], recv_sem=xr_sem.at[kind, step],
            device_id={"front": to}, device_id_type=MESH,
        )

    def arrival(src, dst, kind, step):
        came = lax.rem(front + NFRONT - step, NFRONT)
        return pltpu.make_async_remote_copy(
            src_ref=src.at[came], dst_ref=dst.at[came],
            send_sem=xs_sem.at[kind, step], recv_sem=xr_sem.at[kind, step],
            device_id={"front": came}, device_id_type=MESH,
        )

    def send_first(step, carry):
        exchange(send_i, got_i, 0, step).start()
        exchange(send_p, got_p, 1, step).start()
        return carry

    lax.fori_loop(1, NFRONT, send_first, 0)
    own_i = pltpu.make_async_copy(send_i.at[front], got_i.at[front], own_sem.at[0])
    own_p = pltpu.make_async_copy(send_p.at[front], got_p.at[front], own_sem.at[1])
    own_i.start()
    own_p.start()

    def pack_trail(to, carry):
        for slot in range(CAP):
            pick, _ = choose(to, slot)
            send_t[to, slot * BR : (slot + 1) * BR, :] = blocks_ref[pick, :, PB:]
        return carry

    lax.fori_loop(0, NFRONT, pack_trail, 0)

    def send_second(step, carry):
        exchange(send_t, got_t, 2, step).start()
        return carry

    lax.fori_loop(1, NFRONT, send_second, 0)
    own_t = pltpu.make_async_copy(send_t.at[front], got_t.at[front], own_sem.at[2])
    own_t.start()

    load.wait()
    own_i.wait()
    own_p.wait()

    def take_first(step, carry):
        arrival(send_i, got_i, 0, step).wait_recv()
        arrival(send_p, got_p, 1, step).wait_recv()
        return carry

    lax.fori_loop(1, NFRONT, take_first, 0)

    pieces = []
    for q in range(NFRONT // 4):
        piece = got_i[4 * q, 0:1, :]
        for s in range(1, 4):
            piece = piece + got_i[4 * q + s, 0:1, :]
        pieces.append(piece)
    index = jnp.concatenate(pieces, axis=1)
    index_out[...] = jnp.broadcast_to(index, (8, KALL))
    child = got_p[...].reshape(KALL, PB)
    panel_out[...] = child
    high, low = split(child)
    high, low = high.astype(BF16), low.astype(BF16)

    def assemble(tile, carry):
        base = pl.multiple_of(tile * NB, NB)
        at = lax.broadcasted_iota(jnp.int32, (NB, KALL), 0) + base
        onehot = jnp.where(at == index, 1.0, 0.0).astype(BF16)
        add = dot(onehot, high, NN) + dot(onehot, low, NN)
        part[pl.ds(base, NB), :] = part[pl.ds(base, NB), :] + add
        return carry

    lax.fori_loop(0, rest // NB, assemble, 0)

    half = WIN // 2
    give = pltpu.make_async_remote_copy(
        src_ref=part.at[pl.ds(PB + (1 - core) * half, half), :], dst_ref=pre_win,
        send_sem=pw_sem.at[0], recv_sem=pw_sem.at[1], device_id={"grp": partner}, device_id_type=MESH,
    )
    give.start()

    pivot = part[0:PB, :]
    sym = 0.5 * (pivot + pivot.T)
    sym_out[...] = sym
    table[...] = sym

    owner = owner_ref[0]
    owner_chip = owner // 2
    own_me = owner == group
    own_pair = owner == partner
    shift_right = lax.rem(chip - owner_chip + NCHIP, NCHIP)
    shift_left = lax.rem(owner_chip - chip + NCHIP, NCHIP)

    def ring(way, turn):
        to = 2 * lax.rem(chip + (1 if way == 0 else NCHIP - 1), NCHIP) + core
        return pltpu.make_async_remote_copy(
            src_ref=ring_out.at[way, turn], dst_ref=ring_in.at[way, turn],
            send_sem=rs_sem.at[way, turn], recv_sem=rr_sem.at[way, turn],
            device_id={"grp": to}, device_id_type=MESH,
        )

    def pair(way, turn):
        return pltpu.make_async_remote_copy(
            src_ref=ring_out.at[way, turn], dst_ref=pair_in.at[way, turn],
            send_sem=ps_sem.at[way, turn], recv_sem=pr_sem.at[way, turn],
            device_id={"grp": partner}, device_id_type=MESH,
        )

    def window_turn(turn):
        if turn == 0:
            give.wait_recv()
        for way in range(2):
            if turn > 0:
                ring(way, turn - 1).wait_recv()
            if turn < CHUNKS:
                at = way * (half // 2) + turn * PIECE
                value = part[pl.ds(PB + core * half + at, PIECE), :]
                value = jnp.where(own_me, value, pre_win[pl.ds(at, PIECE), :])
                if turn > 0:
                    value = jnp.where(own_me | own_pair, value, ring_in[way, turn - 1])
            else:
                value = ring_in[way, turn - 1]
            ring_out[way, turn] = value
            if turn < TURNS - 1:
                ring(way, turn).start()
            pair(way, turn).start()

    def width(k):
        return NB * (k + 1)

    def pair_rows(k):
        return pltpu.make_async_remote_copy(
            src_ref=table.at[pl.ds(k * NB + (1 - core) * (NB // 2), NB // 2), pl.ds(0, width(k))],
            dst_ref=pre_w.at[k, :, pl.ds(0, width(k))],
            send_sem=qs_sem.at[k], recv_sem=qr_sem.at[k], device_id={"grp": partner}, device_id_type=MESH,
        )

    def far_rows(k, step):
        to = 2 * lax.rem(chip + step, NCHIP) + core
        return pltpu.make_async_remote_copy(
            src_ref=chip_w.at[k, :, pl.ds(0, width(k))], dst_ref=far_w.at[step - 1, k, :, pl.ds(0, width(k))],
            send_sem=fs_sem.at[step - 1, k], recv_sem=fr_sem.at[step - 1, k],
            device_id={"grp": to}, device_id_type=MESH,
        )

    def back_rows(k):
        return pltpu.make_async_remote_copy(
            src_ref=half_w.at[k, :, pl.ds(0, width(k))], dst_ref=pair_w.at[k, :, pl.ds(0, width(k))],
            send_sem=hs_sem.at[k], recv_sem=hr_sem.at[k], device_id={"grp": partner}, device_id_type=MESH,
        )

    def spread_a(k):
        pair_rows(k).start()

    def spread_b(k):
        pair_rows(k).wait_recv()
        cols = pl.ds(0, width(k))
        own = table[pl.ds(k * NB + core * (NB // 2), NB // 2), cols]
        chip_w[k, :, cols] = jnp.where(own_me, own, pre_w[k, :, cols])
        for step in range(1, NCHIP):
            far_rows(k, step).start()

    def spread_c(k):
        cols = pl.ds(0, width(k))
        value = chip_w[k, :, cols]
        for step in range(1, NCHIP):
            far_rows(k, step).wait_recv()
            value = jnp.where(shift_right == step, far_w[step - 1, k, :, cols], value)
        half_w[k, :, cols] = value
        back_rows(k).start()
        w_out[pl.ds(k * NB + core * (NB // 2), NB // 2), cols] = value

    def spread_d(k):
        back_rows(k).wait_recv()
        cols = pl.ds(0, width(k))
        w_out[pl.ds(k * NB + (1 - core) * (NB // 2), NB // 2), cols] = pair_w[k, :, cols]

    w_out[...] = jnp.zeros_like(w_out)

    def after(k, ib):
        if k == 0 and ib == 1:
            window_turn(0)
        if ib == 5:
            window_turn(2 * k + 1)
        if k > 0 and ib == 1:
            window_turn(2 * k)
            spread_b(k - 1)
        if k > 1 and ib == 3:
            spread_c(k - 2)
        if k > 1 and ib == 7:
            spread_d(k - 2)

    wide = lax.broadcasted_iota(jnp.int32, (NB, PB), 1)
    for k in range(STEPS):
        base = k * NB
        diag[...] = table[base : base + NB, base : base + NB]
        for ib in range(NB // SB):
            eliminate(diag, ib)
            after(k, ib)
        inverse = jnp.where(
            lax.broadcasted_iota(jnp.int32, (NB, NB), 0) >= lax.broadcasted_iota(jnp.int32, (NB, NB), 1),
            diag[...], 0.0,
        )
        above = table[base : base + NB, :]
        above = jnp.where((wide >= base) & (wide < base + NB), 0.0, above)
        reduced = dot3(inverse, above, NN)
        table[base : base + NB, :] = reduced
        table[base : base + NB, base : base + NB] = inverse
        spread_a(k)
        if k + 1 < STEPS:
            upper = table[base : base + NB, :]
            left = reduced[:, base + NB :]
            update = dot3(left, upper, TN)
            old = table[base + NB :, :]
            col = lax.broadcasted_iota(jnp.int32, old.shape, 1)
            old = jnp.where((col >= base) & (col < base + NB), 0.0, old)
            table[base + NB :, :] = old - update

    window_turn(8)
    spread_b(3)
    spread_c(2)
    window_turn(9)
    spread_c(3)
    spread_d(2)

    for way in range(2):
        pair(way, 0).wait_recv()
        shift = shift_right if way == 0 else shift_left
        for turn in range(1, TURNS):
            pair(way, turn).wait_recv()
        for m in range(CHUNKS):
            at = way * (half // 2) + m * PIECE
            own, other = ring_out[way, m], pair_in[way, m]
            for step in range(1, NCHIP):
                own = jnp.where(shift == step, ring_out[way, m + step], own)
                other = jnp.where(shift == step, pair_in[way, m + step], other)
            win_out[pl.ds(core * half + at, PIECE), :] = own
            win_out[pl.ds((1 - core) * half + at, PIECE), :] = other

    own_t.wait()

    def take_second(step, carry):
        arrival(send_t, got_t, 2, step).wait_recv()
        return carry

    lax.fori_loop(1, NFRONT, take_second, 0)
    trail_out[...] = got_t[...].reshape(KALL, WIN)
    spread_d(3)

    def sent(step, carry):
        exchange(send_i, got_i, 0, step).wait_send()
        exchange(send_p, got_p, 1, step).wait_send()
        exchange(send_t, got_t, 2, step).wait_send()
        return carry

    lax.fori_loop(1, NFRONT, sent, 0)
    give.wait_send()
    for way in range(2):
        for turn in range(TURNS):
            if turn < TURNS - 1:
                ring(way, turn).wait_send()
            pair(way, turn).wait_send()
    for k in range(STEPS):
        pair_rows(k).wait_send()
        back_rows(k).wait_send()
        for step in range(1, NCHIP):
            far_rows(k, step).wait_send()


def gather(front_block, blocks, rows, dest, owner):
    vmem = pl.BlockSpec(memory_space=pltpu.VMEM)
    smem = pl.BlockSpec(memory_space=pltpu.SMEM)
    dma = pltpu.SemaphoreType.DMA
    out = [
        jax.ShapeDtypeStruct((WIN, PB), F32),
        jax.ShapeDtypeStruct((PB, PB), F32),
        jax.ShapeDtypeStruct((PB, PB), F32),
        jax.ShapeDtypeStruct((KALL, PB), F32),
        jax.ShapeDtypeStruct((KALL, WIN), F32),
        jax.ShapeDtypeStruct((8, KALL), jnp.int32),
    ]
    return pl.pallas_call(
        gather_kernel,
        out_shape=out,
        in_specs=[pl.BlockSpec(memory_space=pl.ANY), vmem, vmem, smem, smem],
        out_specs=[vmem] * 6,
        scratch_shapes=[
            pltpu.VMEM((PB + WIN, PB), F32),
            pltpu.VMEM((8, 128), jnp.int32),
            pltpu.VMEM((NFRONT, SLOT, PB), F32),
            pltpu.VMEM((NFRONT, SLOT, WIN), F32),
            pltpu.VMEM((NFRONT, 8, 128), jnp.int32),
            pltpu.VMEM((NFRONT, SLOT, PB), F32),
            pltpu.VMEM((NFRONT, SLOT, WIN), F32),
            pltpu.VMEM((NFRONT, 8, 128), jnp.int32),
            pltpu.VMEM((PB, PB), F32),
            pltpu.VMEM((NB, NB), F32),
            pltpu.VMEM((WIN // 2, PB), F32),
            pltpu.VMEM((2, TURNS, PIECE, PB), F32),
            pltpu.VMEM((2, TURNS, PIECE, PB), F32),
            pltpu.VMEM((2, TURNS, PIECE, PB), F32),
            pltpu.VMEM((STEPS, NB // 2, PB), F32),
            pltpu.VMEM((STEPS, NB // 2, PB), F32),
            pltpu.VMEM((NCHIP - 1, STEPS, NB // 2, PB), F32),
            pltpu.VMEM((STEPS, NB // 2, PB), F32),
            pltpu.VMEM((STEPS, NB // 2, PB), F32),
            dma, dma((3,)), dma((3, NFRONT)), dma((3, NFRONT)), dma((2,)),
            dma((2, TURNS)), dma((2, TURNS)), dma((2, TURNS)), dma((2, TURNS)),
            dma((STEPS,)), dma((STEPS,)), dma((NCHIP - 1, STEPS)), dma((NCHIP - 1, STEPS)),
            dma((STEPS,)), dma((STEPS,)),
        ],
        compiler_params=pltpu.CompilerParams(
            collective_id=0, has_side_effects=True, vmem_limit_bytes=56 * 2**20
        ),
        name="gather",
    )(front_block, blocks, rows, dest, owner)


TILE = 256


def finish_kernel(
    owner_ref, a_ref, cp_ref, ct_ref, idx_ref, w_ref, win_ref, sym_ref, panel_ref, schur_ref,
    wh, wl, vh, vl, ph, pw, th, tw,
):
    step = pl.program_id(0)

    @pl.when(step == 0)
    def _():
        high, low = split(w_ref[...])
        wh[...] = high.astype(BF16)
        wl[...] = low.astype(BF16)
        for base in range(0, WIN, 128):
            raw_h, raw_l = split(win_ref[base : base + 128, :])
            solved = dot(raw_h, wh[...], NT) + (dot(raw_h, wl[...], NT) + dot(raw_l, wh[...], NT))
            high, low = split(solved)
            vh[base : base + 128, :] = high.astype(BF16)
            vl[base : base + 128, :] = low.astype(BF16)
        high, low = split(cp_ref[...])
        ph[...] = high.astype(BF16)
        pw[...] = low.astype(BF16)
        high, low = split(ct_ref[...])
        th[...] = high.astype(BF16)
        tw[...] = low.astype(BF16)

    at = lax.broadcasted_iota(jnp.int32, (TILE, KALL), 0) + step * TILE
    onehot = jnp.where(at == idx_ref[0:1, :], 1.0, 0.0).astype(BF16)
    left = a_ref[0, :, 0:PB] + (dot(onehot, ph[...], NN) + dot(onehot, pw[...], NN))
    lh, ll = split(left)
    solved = dot(lh, wh[...], NT) + (dot(lh, wl[...], NT) + dot(ll, wh[...], NT))
    panel_ref[0] = solved
    sh, sl = split(solved)
    right = a_ref[0, :, PB:] + (dot(onehot, th[...], NN) + dot(onehot, tw[...], NN))
    product = dot(sh, vh[...], NT) + (dot(sh, vl[...], NT) + dot(sl, vh[...], NT))
    schur_ref[0] = right - product

    @pl.when((step < PB // TILE) & (owner_ref[0] == owner_ref[1]))
    def _():
        top = pl.multiple_of(step * TILE, TILE)
        gh, gl = split(sym_ref[pl.ds(top, TILE), :])
        factor = dot(gh, wh[...], NT) + (dot(gh, wl[...], NT) + dot(gl, wh[...], NT))
        row = lax.broadcasted_iota(jnp.int32, (TILE, PB), 0) + top
        panel_ref[0] = jnp.where(row >= lax.broadcasted_iota(jnp.int32, (TILE, PB), 1), factor, 0.0)


def finish(owner2, front_block, cp, ct, index, w, window, sym):
    rows = front_block.shape[1]
    smem = pl.BlockSpec(memory_space=pltpu.SMEM)

    def whole(x):
        return pl.BlockSpec(x.shape, lambda i: (0, 0), pipeline_mode=pl.Buffered(1))

    return pl.pallas_call(
        finish_kernel,
        grid=(rows // TILE,),
        out_shape=[jax.ShapeDtypeStruct((1, rows, PB), F32), jax.ShapeDtypeStruct((1, rows, WIN), F32)],
        in_specs=[smem, pl.BlockSpec((1, TILE, PB + WIN), lambda i: (0, i, 0))]
        + [whole(x) for x in (cp, ct, index, w, window, sym)],
        out_specs=[
            pl.BlockSpec((1, TILE, PB), lambda i: (0, i, 0)),
            pl.BlockSpec((1, TILE, WIN), lambda i: (0, i, 0)),
        ],
        scratch_shapes=[
            pltpu.VMEM((PB, PB), BF16), pltpu.VMEM((PB, PB), BF16),
            pltpu.VMEM((WIN, PB), BF16), pltpu.VMEM((WIN, PB), BF16),
            pltpu.VMEM((KALL, PB), BF16), pltpu.VMEM((KALL, PB), BF16),
            pltpu.VMEM((KALL, WIN), BF16), pltpu.VMEM((KALL, WIN), BF16),
        ],
        compiler_params=pltpu.CompilerParams(vmem_limit_bytes=56 * 2**20),
        name="finish",
    )(owner2, front_block, cp, ct, index, w, window, sym)


def local(front_block, child_blocks, child_rows, child_dest, panel_owner):
    window, w, sym, cp, ct, index = gather(
        front_block, child_blocks[0, 0], child_rows[0, 0], child_dest.reshape(KB), panel_owner
    )
    owner2 = jnp.concatenate([panel_owner, lax.axis_index("grp").astype(jnp.int32)[None]])
    return tuple(finish(owner2, front_block, cp, ct, index, w, window, sym))


def solution(mesh):
    placed = (
        P("front", "grp", None),
        P("front", "grp", None, None, None),
        P("front", "grp", None, None),
        P("front", "grp", None, None),
        P("front"),
    )
    return jax.shard_map(
        local,
        mesh=mesh,
        in_specs=placed,
        out_specs=(P("front", "grp", None), P("front", "grp", None)),
        check_vma=False,
    )
```

```python
import functools

import jax
import jax.numpy as jnp
from jax import lax
from jax.experimental import pallas as pl
from jax.experimental.pallas import tpu as pltpu
from jax.sharding import PartitionSpec as P

F32, BF16 = jnp.float32, jnp.bfloat16
MESH = pl.DeviceIdType.MESH
PB, WIN, KB, BR, CAP = 512, 896, 4, 16, 2
NFRONT, NCHIP = 16, 4
SLOT = CAP * BR
KALL = NFRONT * SLOT
NB = 128
STEPS = PB // NB
SB = 16
HALVES = 2

NN = (((1,), (0,)), ((), ()))
NT = (((1,), (1,)), ((), ()))
TN = (((0,), (0,)), ((), ()))


def split(x):
    high = x.astype(BF16).astype(F32)
    return high, x - high


def dot(a, b, dims):
    return lax.dot_general(a.astype(BF16), b.astype(BF16), dims, preferred_element_type=F32)


def dot3(a, b, dims):
    ah, al = split(a)
    bh, bl = split(b)
    return dot(ah, bh, dims) + (dot(ah, bl, dims) + dot(al, bh, dims))


def eliminate(d_ref, k):
    n, b, c0 = NB, SB, k * SB
    lane = lax.broadcasted_iota(jnp.int32, (1, n), 1)
    rows = [d_ref[pl.ds(c0 + i, 1), :] for i in range(b)]
    s = [[None] * b for _ in range(b)]
    for j in range(b):
        for i in range(j, b):
            s[i][j] = jnp.broadcast_to(rows[j][:, c0 + i : c0 + i + 1], (1, n))
    inside = (lane >= c0) & (lane < c0 + b)
    rows = [jnp.where(inside, jnp.where(lane == c0 + i, 1.0, 0.0), rows[i]) for i in range(b)]
    for j in range(b):
        inv = lax.rsqrt(s[j][j])
        for i in range(j + 1, b):
            s[i][j] = s[i][j] * inv
        rows[j] = rows[j] * inv
        for i in range(j + 1, b):
            for q in range(j + 1, i + 1):
                s[i][q] = s[i][q] - s[i][j] * s[q][j]
        for i in range(j + 1, b):
            rows[i] = rows[i] - s[i][j] * rows[j]
        d_ref[pl.ds(c0 + j, 1), :] = rows[j]
    if c0 + b < n:
        u = d_ref[pl.ds(c0, b), :]
        col = lax.broadcasted_iota(jnp.int32, (b, n), 1)
        left = jnp.where(col >= c0 + b, u, 0.0)
        uh, ul = split(u)
        lh, ll = split(left)
        update = dot(jnp.concatenate([lh, lh, ll], 0), jnp.concatenate([uh, ul, uh], 0), TN)
        below = n - c0 - b
        old = d_ref[pl.ds(c0 + b, below), :]
        col = lax.broadcasted_iota(jnp.int32, (below, n), 1)
        old = jnp.where((col >= c0) & (col < c0 + b), 0.0, old)
        d_ref[pl.ds(c0 + b, below), :] = old - update[c0 + b :, :]


HOPS = [(dx, dz) for dx in range(4) for dz in range(4)][1:]
HOPS.sort(key=lambda p: -(min(p[0], 4 - p[0]) + min(p[1], 4 - p[1])))
TILE_A = 256


class Spread:
    def __init__(self, ids, flags, src, full, base, rows, width, pre, cand, part, sems):
        self.chip, self.core, self.partner = ids
        self.own_me, self.shift = flags
        self.src, self.full, self.base, self.rows, self.width = src, full, base, rows, width
        self.pre, self.cand, self.part, self.sems = pre, cand, part, sems

    def copy(self, src, dst, sem, to):
        return pltpu.make_async_remote_copy(
            src_ref=src, dst_ref=dst, send_sem=self.sems.at[2 * sem], recv_sem=self.sems.at[2 * sem + 1],
            device_id={"grp": to}, device_id_type=MESH,
        )

    def cut(self, ref, start, size):
        return ref.at[pl.ds(start, size), pl.ds(0, self.width)]

    def other(self, step):
        return lax.rem(self.chip + step, NCHIP)

    def first(self):
        half = self.rows // 2
        return self.copy(
            self.cut(self.src[0], self.src[1] + (1 - self.core) * half, half), self.cut(self.pre, 0, half), 0, self.partner
        )

    def second(self, step):
        size = self.rows // 8
        to = self.other(step)
        return self.copy(
            self.cut(self.cand, to * size, size),
            self.part.at[step - 1, :, pl.ds(0, self.width)], step, 2 * to + self.core,
        )

    def third(self, step):
        size = self.rows // 8
        at = self.base + self.core * (self.rows // 2) + self.chip * size
        return self.copy(
            self.cut(self.full, at, size), self.cut(self.full, at, size), NCHIP - 1 + step, 2 * self.other(step) + self.core
        )

    def fourth(self):
        half = self.rows // 2
        at = self.base + self.core * half
        return self.copy(self.cut(self.full, at, half), self.cut(self.full, at, half), 2 * NCHIP - 1, self.partner)

    def pairs(self):
        self.first().start()

    def scatter(self):
        self.first().wait_recv()
        half, cols = self.rows // 2, pl.ds(0, self.width)
        own = self.src[0][pl.ds(self.src[1] + self.core * half, half), cols]
        self.cand[:, cols] = jnp.where(self.own_me, own, self.pre[:, cols])
        for step in range(1, NCHIP):
            self.second(step).start()

    def collect(self):
        size, cols = self.rows // 8, pl.ds(0, self.width)
        value = self.cand[pl.ds(self.chip * size, size), cols]
        for step in range(1, NCHIP):
            self.second(step).wait_recv()
            value = jnp.where(self.shift == step, self.part[step - 1, :, cols], value)
        self.full[pl.ds(self.base + self.core * (self.rows // 2) + self.chip * size, size), cols] = value
        for step in range(1, NCHIP):
            self.third(step).start()

    def back(self):
        for step in range(1, NCHIP):
            self.third(step).wait_recv()
        self.fourth().start()

    def end(self):
        self.fourth().wait_recv()

    def sent(self):
        self.first().wait_send()
        self.fourth().wait_send()
        for step in range(1, NCHIP):
            self.second(step).wait_send()
            self.third(step).wait_send()


def gather_kernel(
    front_ref, blocks_ref, rows_ref, dest_ref, owner_ref,
    panel_out, trail_out, win_out, w_out, sym_out,
    part, trail, rowbuf, send_p, send_t, send_i, got_p, got_t, got_i,
    table, symm, diag, high_t, low_t, win_pre, win_cand, win_part, win_full, w_pre, w_cand, w_part, w_full,
    load_sem, own_sem, xs_sem, xr_sem, win_sem, w_sem, out_sem,
):
    front = lax.axis_index("front")
    group = lax.axis_index("grp")
    chip, core = group // 2, group % 2
    x, z = front // 4, front % 4
    rest = PB + WIN
    total = front_ref.shape[1]

    loads = [
        pltpu.make_async_copy(front_ref.at[0, pl.ds(0, total), pl.ds(0, PB)], part, load_sem.at[0]),
        pltpu.make_async_copy(front_ref.at[0, pl.ds(0, total), pl.ds(PB, WIN)], trail, load_sem.at[1]),
    ]
    loads[0].start()

    barrier = pltpu.get_barrier_semaphore()

    def after_me(hop):
        return lax.rem(x + hop[0], 4) * 4 + lax.rem(z + hop[1], 4)

    def before_me(hop):
        return lax.rem(x + 4 - hop[0], 4) * 4 + lax.rem(z + 4 - hop[1], 4)

    for hop in HOPS:
        pl.semaphore_signal(barrier, inc=1, device_id={"front": after_me(hop)}, device_id_type=MESH)
    partner = 2 * chip + (1 - core)
    pl.semaphore_signal(barrier, inc=1, device_id={"grp": partner}, device_id_type=MESH)
    for step in range(1, NCHIP):
        there = 2 * lax.rem(chip + step, NCHIP) + core
        pl.semaphore_signal(barrier, inc=1, device_id={"grp": there}, device_id_type=MESH)

    rowbuf[...] = jnp.zeros_like(rowbuf)
    rowbuf[0:KB, 0:BR] = rows_ref[...]
    spread = rowbuf[...]
    for width in (16, 32, 64):
        spread = spread + pltpu.roll(spread, width, 1)
    rowbuf[...] = spread
    dests = [dest_ref[k] for k in range(KB)]
    ranks = []
    for k in range(KB):
        rank = jnp.int32(0)
        for e in range(k):
            rank = rank + (dests[e] == dests[k]).astype(jnp.int32)
        ranks.append(rank)
    lane = lax.broadcasted_iota(jnp.int32, (8, 128), 1)
    mine = lax.rem(front, 4) * SLOT

    def choose(to, slot):
        pick, found = jnp.int32(0), jnp.int32(0)
        for k in range(KB):
            hit = ((dests[k] == to) & (ranks[k] == slot)).astype(jnp.int32)
            pick = pick + hit * k
            found = found + hit
        return pick, found

    def pack_panel(to, carry):
        index = jnp.zeros((8, 128), jnp.int32)
        for slot in range(CAP):
            pick, found = choose(to, slot)
            send_p[to, slot * BR : (slot + 1) * BR, :] = blocks_ref[pick, :, 0:PB]
            at = jnp.broadcast_to(rowbuf[pl.ds(pick, 1), :], (8, 128))
            at = jnp.where(found > 0, at, -1)
            base = mine + slot * BR
            index = jnp.where((lane >= base) & (lane < base + BR), at, index)
        send_i[to] = index
        return carry

    lax.fori_loop(0, NFRONT, pack_panel, 0)
    pl.semaphore_wait(barrier, NFRONT - 1 + 1 + NCHIP - 1)

    def exchange(src, dst, kind, n):
        to = after_me(HOPS[n])
        return pltpu.make_async_remote_copy(
            src_ref=src.at[to], dst_ref=dst.at[front],
            send_sem=xs_sem.at[kind, n], recv_sem=xr_sem.at[kind, n],
            device_id={"front": to}, device_id_type=MESH,
        )

    def arrival(src, dst, kind, n):
        came = before_me(HOPS[n])
        return pltpu.make_async_remote_copy(
            src_ref=src.at[came], dst_ref=dst.at[came],
            send_sem=xs_sem.at[kind, n], recv_sem=xr_sem.at[kind, n],
            device_id={"front": came}, device_id_type=MESH,
        )

    for n in range(NFRONT - 1):
        exchange(send_i, got_i, 0, n).start()
        exchange(send_p, got_p, 1, n).start()
    owns = [
        pltpu.make_async_copy(send_i.at[front], got_i.at[front], own_sem.at[0]),
        pltpu.make_async_copy(send_p.at[front], got_p.at[front], own_sem.at[1]),
        pltpu.make_async_copy(send_t.at[front], got_t.at[front], own_sem.at[2]),
    ]
    owns[0].start()
    owns[1].start()
    loads[1].start()

    def pack_trail(to, carry):
        for slot in range(CAP):
            pick, _ = choose(to, slot)
            send_t[to, slot * BR : (slot + 1) * BR, :] = blocks_ref[pick, :, PB:]
        return carry

    lax.fori_loop(0, NFRONT, pack_trail, 0)
    for n in range(NFRONT - 1):
        exchange(send_t, got_t, 2, n).start()
    owns[2].start()

    loads[0].wait()
    owns[0].wait()
    owns[1].wait()
    for n in range(NFRONT - 1):
        arrival(send_i, got_i, 0, n).wait_recv()
        arrival(send_p, got_p, 1, n).wait_recv()

    pieces = []
    for q in range(NFRONT // 4):
        piece = got_i[4 * q, 0:1, :]
        for s in range(1, 4):
            piece = piece + got_i[4 * q + s, 0:1, :]
        pieces.append(piece)
    index = jnp.concatenate(pieces, axis=1)
    high, low = split(got_p[...].reshape(KALL, PB))
    high, low = high.astype(BF16), low.astype(BF16)

    def onehot(base, size):
        at = lax.broadcasted_iota(jnp.int32, (size, KALL), 0) + base
        return jnp.where(at == index, 1.0, 0.0).astype(BF16)

    def assemble(tile, carry):
        base = pl.multiple_of(tile * TILE_A, TILE_A)
        at = onehot(base, TILE_A)
        part[pl.ds(base, TILE_A), :] = part[pl.ds(base, TILE_A), :] + (dot(at, high, NN) + dot(at, low, NN))
        return carry

    lax.fori_loop(0, total // TILE_A, assemble, 0)
    outs = [pltpu.make_async_copy(part, panel_out, out_sem.at[0])]
    outs[0].start()

    owner = owner_ref[0]
    ids = (chip, core, partner)
    flags = (owner == group, lax.rem(chip - owner // 2 + NCHIP, NCHIP))
    size = WIN // HALVES
    window = [
        Spread(ids, flags, (part, PB + h * size), win_full, h * size, size, PB,
               win_pre.at[h], win_cand.at[h], win_part.at[h], win_sem.at[h])
        for h in range(HALVES)
    ]
    inverse_rows = [
        Spread(ids, flags, (table, k * NB), w_full, k * NB, NB, NB * (k + 1),
               w_pre.at[k], w_cand.at[k], w_part.at[k], w_sem.at[k])
        for k in range(STEPS)
    ]
    for one in window:
        one.pairs()

    pivot = part[0:PB, :]
    sym = 0.5 * (pivot + pivot.T)
    symm[...] = sym
    table[...] = sym
    outs.append(pltpu.make_async_copy(symm, sym_out, out_sem.at[1]))
    outs[1].start()
    w_full[...] = jnp.zeros_like(w_full)

    plan = {
        (0, 0): [window[0].scatter],
        (0, 1): [window[1].scatter],
        (1, 2): [inverse_rows[0].scatter],
        (1, 3): [window[0].collect],
        (2, 1): [inverse_rows[0].collect],
        (2, 2): [inverse_rows[1].scatter],
        (2, 4): [window[1].collect],
        (3, 1): [inverse_rows[0].back],
        (3, 2): [inverse_rows[2].scatter],
        (3, 3): [inverse_rows[1].collect],
        (3, 5): [window[0].back],
    }

    wide = lax.broadcasted_iota(jnp.int32, (NB, PB), 1)
    for k in range(STEPS):
        base = k * NB
        diag[...] = table[base : base + NB, base : base + NB]
        for ib in range(NB // SB):
            eliminate(diag, ib)
            for task in plan.get((k, ib), ()):
                task()
        inverse = jnp.where(
            lax.broadcasted_iota(jnp.int32, (NB, NB), 0) >= lax.broadcasted_iota(jnp.int32, (NB, NB), 1),
            diag[...], 0.0,
        )
        above = table[base : base + NB, :]
        above = jnp.where((wide >= base) & (wide < base + NB), 0.0, above)
        reduced = dot3(inverse, above, NN)
        table[base : base + NB, :] = reduced
        table[base : base + NB, base : base + NB] = inverse
        inverse_rows[k].pairs()
        if k + 1 < STEPS:
            upper = table[base : base + NB, :]
            left = reduced[:, base + NB :]
            update = dot3(left, upper, TN)
            old = table[base + NB :, :]
            col = lax.broadcasted_iota(jnp.int32, old.shape, 1)
            old = jnp.where((col >= base) & (col < base + NB), 0.0, old)
            table[base + NB :, :] = old - update

    inverse_rows[3].scatter()
    inverse_rows[2].collect()
    inverse_rows[1].back()

    loads[1].wait()
    owns[2].wait()
    for n in range(NFRONT - 1):
        arrival(send_t, got_t, 2, n).wait_recv()
    head, tail = split(got_t[...].reshape(KALL, WIN))
    high_t[...] = head.astype(BF16)
    low_t[...] = tail.astype(BF16)

    def add_trail(tile, carry):
        base = pl.multiple_of(tile * TILE_A, TILE_A)
        at = onehot(base, TILE_A)
        trail[pl.ds(base, TILE_A), :] = trail[pl.ds(base, TILE_A), :] + (
            dot(at, high_t[...], NN) + dot(at, low_t[...], NN)
        )
        return carry

    tiles = total // TILE_A
    cuts = [0, 3 * tiles // 8, 6 * tiles // 8, tiles]
    tasks = [
        [inverse_rows[3].collect, inverse_rows[2].back],
        [window[1].back, inverse_rows[3].back],
        [],
    ]
    for part_at in range(3):
        lax.fori_loop(cuts[part_at], cuts[part_at + 1], add_trail, 0)
        rows = pl.ds(cuts[part_at] * TILE_A, (cuts[part_at + 1] - cuts[part_at]) * TILE_A)
        outs.append(pltpu.make_async_copy(trail.at[rows, :], trail_out.at[rows, :], out_sem.at[2 + part_at]))
        outs[-1].start()
        for task in tasks[part_at]:
            task()

    for one in window:
        one.end()
    outs.append(pltpu.make_async_copy(win_full, win_out, out_sem.at[5]))
    outs[-1].start()
    for one in inverse_rows:
        one.end()
    outs.append(pltpu.make_async_copy(w_full, w_out, out_sem.at[6]))
    outs[-1].start()

    for n in range(NFRONT - 1):
        exchange(send_i, got_i, 0, n).wait_send()
        exchange(send_p, got_p, 1, n).wait_send()
        exchange(send_t, got_t, 2, n).wait_send()
    for one in window + inverse_rows:
        one.sent()
    for one in outs:
        one.wait()


def gather(front_block, blocks, rows, dest, owner):
    vmem = pl.BlockSpec(memory_space=pltpu.VMEM)
    smem = pl.BlockSpec(memory_space=pltpu.SMEM)
    hbm = pl.BlockSpec(memory_space=pl.ANY)
    dma = pltpu.SemaphoreType.DMA
    total = front_block.shape[1]
    size = WIN // HALVES

    def buf(*shape, dtype=F32):
        return pltpu.VMEM(shape, dtype)

    return pl.pallas_call(
        gather_kernel,
        out_shape=[
            jax.ShapeDtypeStruct((total, PB), F32),
            jax.ShapeDtypeStruct((total, WIN), F32),
            jax.ShapeDtypeStruct((WIN, PB), F32),
            jax.ShapeDtypeStruct((PB, PB), F32),
            jax.ShapeDtypeStruct((PB, PB), F32),
        ],
        in_specs=[hbm, vmem, vmem, smem, smem],
        out_specs=[hbm] * 5,
        scratch_shapes=[
            buf(total, PB), buf(total, WIN), buf(8, 128, dtype=jnp.int32),
            buf(NFRONT, SLOT, PB), buf(NFRONT, SLOT, WIN), buf(NFRONT, 8, 128, dtype=jnp.int32),
            buf(NFRONT, SLOT, PB), buf(NFRONT, SLOT, WIN), buf(NFRONT, 8, 128, dtype=jnp.int32),
            buf(PB, PB), buf(PB, PB), buf(NB, NB),
            buf(KALL, WIN, dtype=BF16), buf(KALL, WIN, dtype=BF16),
            buf(HALVES, size // 2, PB), buf(HALVES, size // 2, PB),
            buf(HALVES, NCHIP - 1, size // 8, PB), buf(WIN, PB),
            buf(STEPS, NB // 2, PB), buf(STEPS, NB // 2, PB),
            buf(STEPS, NCHIP - 1, NB // 8, PB), buf(PB, PB),
            dma((2,)), dma((3,)), dma((3, NFRONT)), dma((3, NFRONT)),
            dma((HALVES, 4 * NCHIP)), dma((STEPS, 4 * NCHIP)), dma((7,)),
        ],
        compiler_params=pltpu.CompilerParams(
            collective_id=0, has_side_effects=True, vmem_limit_bytes=56 * 2**20
        ),
        name="gather",
    )(front_block, blocks, rows, dest, owner)


TILE = 512


def finish_kernel(owner_ref, a_ref, b_ref, w_ref, win_ref, sym_ref, panel_ref, schur_ref, wh, wl, vh, vl):
    step = pl.program_id(0)

    def solve(left):
        lh, ll = split(left)
        lh, ll = lh.astype(BF16), ll.astype(BF16)
        half = PB // 2
        sides = []
        for n, depth in ((0, half), (half, PB)):
            ah, al = lh[:, :depth], ll[:, :depth]
            bh, bl = wh[n : n + half, :depth], wl[n : n + half, :depth]
            sides.append(dot(ah, bh, NT) + (dot(ah, bl, NT) + dot(al, bh, NT)))
        return jnp.concatenate(sides, axis=1)

    @pl.when(step == 0)
    def _():
        high, low = split(w_ref[...])
        wh[...] = high.astype(BF16)
        wl[...] = low.astype(BF16)
        for base in range(0, WIN, 128):
            high, low = split(solve(win_ref[base : base + 128, :]))
            vh[base : base + 128, :] = high.astype(BF16)
            vl[base : base + 128, :] = low.astype(BF16)

    solved = solve(a_ref[...])
    panel_ref[0] = solved
    sh, sl = split(solved)
    product = dot(sh, vh[...], NT) + (dot(sh, vl[...], NT) + dot(sl, vh[...], NT))
    schur_ref[0] = b_ref[...] - product

    @pl.when((step < PB // TILE) & (owner_ref[0] == owner_ref[1]))
    def _():
        top = pl.multiple_of(step * TILE, TILE)
        factor = solve(sym_ref[pl.ds(top, TILE), :])
        row = lax.broadcasted_iota(jnp.int32, (TILE, PB), 0) + top
        panel_ref[0] = jnp.where(row >= lax.broadcasted_iota(jnp.int32, (TILE, PB), 1), factor, 0.0)


def finish(owner2, a, b, w, window, sym):
    rows = a.shape[0]
    smem = pl.BlockSpec(memory_space=pltpu.SMEM)

    def whole(v):
        return pl.BlockSpec(v.shape, lambda i: (0, 0), pipeline_mode=pl.Buffered(1))

    return pl.pallas_call(
        finish_kernel,
        grid=(rows // TILE,),
        out_shape=[jax.ShapeDtypeStruct((1, rows, PB), F32), jax.ShapeDtypeStruct((1, rows, WIN), F32)],
        in_specs=[smem, pl.BlockSpec((TILE, PB), lambda i: (i, 0)), pl.BlockSpec((TILE, WIN), lambda i: (i, 0))]
        + [whole(v) for v in (w, window, sym)],
        out_specs=[
            pl.BlockSpec((1, TILE, PB), lambda i: (0, i, 0)),
            pl.BlockSpec((1, TILE, WIN), lambda i: (0, i, 0)),
        ],
        scratch_shapes=[
            pltpu.VMEM((PB, PB), BF16), pltpu.VMEM((PB, PB), BF16),
            pltpu.VMEM((WIN, PB), BF16), pltpu.VMEM((WIN, PB), BF16),
        ],
        compiler_params=pltpu.CompilerParams(vmem_limit_bytes=56 * 2**20),
        name="finish",
    )(owner2, a, b, w, window, sym)


def local(front_block, child_blocks, child_rows, child_dest, panel_owner):
    panel, trail, window, w, sym = gather(
        front_block, child_blocks[0, 0], child_rows[0, 0], child_dest.reshape(KB), panel_owner
    )
    owner2 = jnp.concatenate([panel_owner, lax.axis_index("grp").astype(jnp.int32)[None]])
    return tuple(finish(owner2, panel, trail, w, window, sym))


def solution(mesh):
    placed = (
        P("front", "grp", None),
        P("front", "grp", None, None, None),
        P("front", "grp", None, None),
        P("front", "grp", None, None),
        P("front"),
    )
    return jax.shard_map(
        local,
        mesh=mesh,
        in_specs=placed,
        out_specs=(P("front", "grp", None), P("front", "grp", None)),
        check_vma=False,
    )
```

```python
import functools

import jax
import jax.numpy as jnp
from jax import lax
from jax.experimental import pallas as pl
from jax.experimental.pallas import tpu as pltpu
from jax.sharding import PartitionSpec as P

F32, BF16 = jnp.float32, jnp.bfloat16
MESH = pl.DeviceIdType.MESH
PB, WIN, KB, BR, CAP = 512, 896, 4, 16, 2
NFRONT, NCHIP = 16, 4
SLOT = CAP * BR
KALL = NFRONT * SLOT
NB = 128
STEPS = PB // NB
SB = 16
HALVES = 2

NN = (((1,), (0,)), ((), ()))
NT = (((1,), (1,)), ((), ()))
TN = (((0,), (0,)), ((), ()))


def split(x):
    high = x.astype(BF16).astype(F32)
    return high, x - high


def dot(a, b, dims):
    return lax.dot_general(a.astype(BF16), b.astype(BF16), dims, preferred_element_type=F32)


def dot3(a, b, dims):
    ah, al = split(a)
    bh, bl = split(b)
    return dot(ah, bh, dims) + (dot(ah, bl, dims) + dot(al, bh, dims))


def eliminate(d_ref, k):
    n, b, c0 = NB, SB, k * SB
    lane = lax.broadcasted_iota(jnp.int32, (1, n), 1)
    rows = [d_ref[pl.ds(c0 + i, 1), :] for i in range(b)]
    s = [[None] * b for _ in range(b)]
    for j in range(b):
        for i in range(j, b):
            s[i][j] = jnp.broadcast_to(rows[j][:, c0 + i : c0 + i + 1], (1, n))
    inside = (lane >= c0) & (lane < c0 + b)
    rows = [jnp.where(inside, jnp.where(lane == c0 + i, 1.0, 0.0), rows[i]) for i in range(b)]
    for j in range(b):
        inv = lax.rsqrt(s[j][j])
        for i in range(j + 1, b):
            s[i][j] = s[i][j] * inv
        rows[j] = rows[j] * inv
        for i in range(j + 1, b):
            for q in range(j + 1, i + 1):
                s[i][q] = s[i][q] - s[i][j] * s[q][j]
        for i in range(j + 1, b):
            rows[i] = rows[i] - s[i][j] * rows[j]
        d_ref[pl.ds(c0 + j, 1), :] = rows[j]
    if c0 + b < n:
        u = d_ref[pl.ds(c0, b), :]
        col = lax.broadcasted_iota(jnp.int32, (b, n), 1)
        left = jnp.where(col >= c0 + b, u, 0.0)
        uh, ul = split(u)
        lh, ll = split(left)
        update = dot(jnp.concatenate([lh, lh, ll], 0), jnp.concatenate([uh, ul, uh], 0), TN)
        below = n - c0 - b
        old = d_ref[pl.ds(c0 + b, below), :]
        col = lax.broadcasted_iota(jnp.int32, (below, n), 1)
        old = jnp.where((col >= c0) & (col < c0 + b), 0.0, old)
        d_ref[pl.ds(c0 + b, below), :] = old - update[c0 + b :, :]


HOPS = [(dx, dz) for dx in range(4) for dz in range(4)][1:]
HOPS.sort(key=lambda p: -(min(p[0], 4 - p[0]) + min(p[1], 4 - p[1])))
TILE_A = 256
FIRST, EVERY = 1, 2


class Spread:
    def __init__(self, ids, flags, src, full, base, rows, width, pre, cand, part, sems):
        self.chip, self.core, self.partner = ids
        self.own_me, self.shift = flags
        self.src, self.full, self.base, self.rows, self.width = src, full, base, rows, width
        self.pre, self.cand, self.part, self.sems = pre, cand, part, sems

    def copy(self, src, dst, sem, to):
        return pltpu.make_async_remote_copy(
            src_ref=src, dst_ref=dst, send_sem=self.sems.at[2 * sem], recv_sem=self.sems.at[2 * sem + 1],
            device_id={"grp": to}, device_id_type=MESH,
        )

    def cut(self, ref, start, size):
        return ref.at[pl.ds(start, size), pl.ds(0, self.width)]

    def other(self, step):
        return lax.rem(self.chip + step, NCHIP)

    def first(self):
        half = self.rows // 2
        return self.copy(
            self.cut(self.src[0], self.src[1] + (1 - self.core) * half, half), self.cut(self.pre, 0, half), 0, self.partner
        )

    def second(self, step):
        size = self.rows // 8
        to = self.other(step)
        return self.copy(
            self.cut(self.cand, to * size, size),
            self.part.at[step - 1, :, pl.ds(0, self.width)], step, 2 * to + self.core,
        )

    def third(self, step):
        size = self.rows // 8
        at = self.base + self.core * (self.rows // 2) + self.chip * size
        return self.copy(
            self.cut(self.full, at, size), self.cut(self.full, at, size), NCHIP - 1 + step, 2 * self.other(step) + self.core
        )

    def fourth(self):
        half = self.rows // 2
        at = self.base + self.core * half
        return self.copy(self.cut(self.full, at, half), self.cut(self.full, at, half), 2 * NCHIP - 1, self.partner)

    def pairs(self):
        self.first().start()

    def scatter(self):
        self.first().wait_recv()
        half, cols = self.rows // 2, pl.ds(0, self.width)
        own = self.src[0][pl.ds(self.src[1] + self.core * half, half), cols]
        self.cand[:, cols] = jnp.where(self.own_me, own, self.pre[:, cols])
        for step in range(1, NCHIP):
            self.second(step).start()

    def collect(self):
        size, cols = self.rows // 8, pl.ds(0, self.width)
        value = self.cand[pl.ds(self.chip * size, size), cols]
        for step in range(1, NCHIP):
            self.second(step).wait_recv()
            value = jnp.where(self.shift == step, self.part[step - 1, :, cols], value)
        self.full[pl.ds(self.base + self.core * (self.rows // 2) + self.chip * size, size), cols] = value
        for step in range(1, NCHIP):
            self.third(step).start()

    def back(self):
        for step in range(1, NCHIP):
            self.third(step).wait_recv()
        self.fourth().start()

    def end(self):
        self.fourth().wait_recv()

    def sent(self):
        self.first().wait_send()
        self.fourth().wait_send()
        for step in range(1, NCHIP):
            self.second(step).wait_send()
            self.third(step).wait_send()


def gather_kernel(
    front_ref, blocks_ref, rows_ref, dest_ref, owner_ref,
    panel_out, trail_out, win_out, w_out, sym_out,
    part, trail, rowbuf, send_p, send_t, send_i, got_p, got_t, got_i,
    table, symm, diag, high_t, low_t, win_pre, win_cand, win_part, win_full, w_pre, w_cand, w_part, w_full,
    load_sem, own_sem, xs_sem, xr_sem, win_sem, w_sem, out_sem,
):
    front = lax.axis_index("front")
    group = lax.axis_index("grp")
    chip, core = group // 2, group % 2
    x, z = front // 4, front % 4
    rest = PB + WIN
    total = front_ref.shape[1]

    loads = [
        pltpu.make_async_copy(front_ref.at[0, pl.ds(0, total), pl.ds(0, PB)], part, load_sem.at[0]),
        pltpu.make_async_copy(front_ref.at[0, pl.ds(0, total), pl.ds(PB, WIN)], trail, load_sem.at[1]),
    ]
    loads[0].start()

    barrier = pltpu.get_barrier_semaphore()

    def after_me(hop):
        return lax.rem(x + hop[0], 4) * 4 + lax.rem(z + hop[1], 4)

    def before_me(hop):
        return lax.rem(x + 4 - hop[0], 4) * 4 + lax.rem(z + 4 - hop[1], 4)

    for hop in HOPS:
        pl.semaphore_signal(barrier, inc=1, device_id={"front": after_me(hop)}, device_id_type=MESH)
    partner = 2 * chip + (1 - core)
    pl.semaphore_signal(barrier, inc=1, device_id={"grp": partner}, device_id_type=MESH)
    for step in range(1, NCHIP):
        there = 2 * lax.rem(chip + step, NCHIP) + core
        pl.semaphore_signal(barrier, inc=1, device_id={"grp": there}, device_id_type=MESH)

    rowbuf[...] = jnp.zeros_like(rowbuf)
    rowbuf[0:KB, 0:BR] = rows_ref[...]
    spread = rowbuf[...]
    for width in (16, 32, 64):
        spread = spread + pltpu.roll(spread, width, 1)
    rowbuf[...] = spread
    dests = [dest_ref[k] for k in range(KB)]
    ranks = []
    for k in range(KB):
        rank = jnp.int32(0)
        for e in range(k):
            rank = rank + (dests[e] == dests[k]).astype(jnp.int32)
        ranks.append(rank)
    lane = lax.broadcasted_iota(jnp.int32, (8, 128), 1)
    mine = lax.rem(front, 4) * SLOT

    def choose(to, slot):
        pick, found = jnp.int32(0), jnp.int32(0)
        for k in range(KB):
            hit = ((dests[k] == to) & (ranks[k] == slot)).astype(jnp.int32)
            pick = pick + hit * k
            found = found + hit
        return pick, found

    def pack_panel(to, carry):
        index = jnp.zeros((8, 128), jnp.int32)
        for slot in range(CAP):
            pick, found = choose(to, slot)
            send_p[to, slot * BR : (slot + 1) * BR, :] = blocks_ref[pick, :, 0:PB]
            at = jnp.broadcast_to(rowbuf[pl.ds(pick, 1), :], (8, 128))
            at = jnp.where(found > 0, at, -1)
            base = mine + slot * BR
            index = jnp.where((lane >= base) & (lane < base + BR), at, index)
        send_i[to] = index
        return carry

    lax.fori_loop(0, NFRONT, pack_panel, 0)
    pl.semaphore_wait(barrier, NFRONT - 1 + 1 + NCHIP - 1)

    def exchange(src, dst, kind, n):
        to = after_me(HOPS[n])
        return pltpu.make_async_remote_copy(
            src_ref=src.at[to], dst_ref=dst.at[front],
            send_sem=xs_sem.at[kind, n], recv_sem=xr_sem.at[kind, n],
            device_id={"front": to}, device_id_type=MESH,
        )

    def arrival(src, dst, kind, n):
        came = before_me(HOPS[n])
        return pltpu.make_async_remote_copy(
            src_ref=src.at[came], dst_ref=dst.at[came],
            send_sem=xs_sem.at[kind, n], recv_sem=xr_sem.at[kind, n],
            device_id={"front": came}, device_id_type=MESH,
        )

    for n in range(NFRONT - 1):
        exchange(send_i, got_i, 0, n).start()
        exchange(send_p, got_p, 1, n).start()
    owns = [
        pltpu.make_async_copy(send_i.at[front], got_i.at[front], own_sem.at[0]),
        pltpu.make_async_copy(send_p.at[front], got_p.at[front], own_sem.at[1]),
        pltpu.make_async_copy(send_t.at[front], got_t.at[front], own_sem.at[2]),
    ]
    owns[0].start()
    owns[1].start()
    loads[1].start()

    def pack_trail(to, carry):
        for slot in range(CAP):
            pick, _ = choose(to, slot)
            send_t[to, slot * BR : (slot + 1) * BR, :] = blocks_ref[pick, :, PB:]
        return carry

    lax.fori_loop(0, NFRONT, pack_trail, 0)
    owns[2].start()

    loads[0].wait()
    owns[0].wait()
    owns[1].wait()
    for n in range(NFRONT - 1):
        arrival(send_i, got_i, 0, n).wait_recv()
        arrival(send_p, got_p, 1, n).wait_recv()

    pieces = []
    for q in range(NFRONT // 4):
        piece = got_i[4 * q, 0:1, :]
        for s in range(1, 4):
            piece = piece + got_i[4 * q + s, 0:1, :]
        pieces.append(piece)
    index = jnp.concatenate(pieces, axis=1)
    high, low = split(got_p[...].reshape(KALL, PB))
    high, low = high.astype(BF16), low.astype(BF16)

    def onehot(base, size):
        at = lax.broadcasted_iota(jnp.int32, (size, KALL), 0) + base
        return jnp.where(at == index, 1.0, 0.0).astype(BF16)

    def assemble(tile, carry):
        base = pl.multiple_of(tile * TILE_A, TILE_A)
        at = onehot(base, TILE_A)
        part[pl.ds(base, TILE_A), :] = part[pl.ds(base, TILE_A), :] + (dot(at, high, NN) + dot(at, low, NN))
        return carry

    lax.fori_loop(0, total // TILE_A, assemble, 0)
    outs = [
        pltpu.make_async_copy(part, panel_out, out_sem.at[0]),
        pltpu.make_async_copy(symm, sym_out, out_sem.at[1]),
    ]

    owner = owner_ref[0]
    ids = (chip, core, partner)
    flags = (owner == group, lax.rem(chip - owner // 2 + NCHIP, NCHIP))
    size = WIN // HALVES
    window = [
        Spread(ids, flags, (part, PB + h * size), win_full, h * size, size, PB,
               win_pre.at[h], win_cand.at[h], win_part.at[h], win_sem.at[h])
        for h in range(HALVES)
    ]
    inverse_rows = [
        Spread(ids, flags, (table, k * NB), w_full, k * NB, NB, NB * (k + 1),
               w_pre.at[k], w_cand.at[k], w_part.at[k], w_sem.at[k])
        for k in range(STEPS)
    ]
    for one in window:
        one.pairs()

    pivot = part[0:PB, :]
    sym = 0.5 * (pivot + pivot.T)
    symm[...] = sym
    table[...] = sym
    w_full[...] = jnp.zeros_like(w_full)

    plan = {
        (0, 1): [window[0].scatter],
        (0, 3): [window[1].scatter],
        (0, 6): [outs[1].start],
        (1, 0): [outs[0].start],
        (1, 2): [inverse_rows[0].scatter],
        (1, 4): [window[0].collect],
        (1, 6): [inverse_rows[0].collect],
        (2, 1): [inverse_rows[0].back],
        (2, 2): [inverse_rows[1].scatter],
        (2, 5): [window[1].collect],
        (2, 6): [inverse_rows[1].collect],
        (3, 0): [window[0].back],
        (3, 1): [inverse_rows[1].back],
        (3, 2): [inverse_rows[2].scatter],
        (3, 6): [inverse_rows[2].collect],
    }
    for n in range(NFRONT - 1):
        at = FIRST + EVERY * n
        plan.setdefault((at // (NB // SB), at % (NB // SB)), []).append(exchange(send_t, got_t, 2, n).start)

    wide = lax.broadcasted_iota(jnp.int32, (NB, PB), 1)
    for k in range(STEPS):
        base = k * NB
        diag[...] = table[base : base + NB, base : base + NB]
        for ib in range(NB // SB):
            eliminate(diag, ib)
            for task in plan.get((k, ib), ()):
                task()
        inverse = jnp.where(
            lax.broadcasted_iota(jnp.int32, (NB, NB), 0) >= lax.broadcasted_iota(jnp.int32, (NB, NB), 1),
            diag[...], 0.0,
        )
        above = table[base : base + NB, :]
        above = jnp.where((wide >= base) & (wide < base + NB), 0.0, above)
        reduced = dot3(inverse, above, NN)
        table[base : base + NB, :] = reduced
        table[base : base + NB, base : base + NB] = inverse
        inverse_rows[k].pairs()
        if k + 1 < STEPS:
            upper = table[base : base + NB, :]
            left = reduced[:, base + NB :]
            update = dot3(left, upper, TN)
            old = table[base + NB :, :]
            col = lax.broadcasted_iota(jnp.int32, old.shape, 1)
            old = jnp.where((col >= base) & (col < base + NB), 0.0, old)
            table[base + NB :, :] = old - update

    inverse_rows[3].scatter()
    inverse_rows[2].back()

    loads[1].wait()
    owns[2].wait()
    for n in range(NFRONT - 1):
        arrival(send_t, got_t, 2, n).wait_recv()
    head, tail = split(got_t[...].reshape(KALL, WIN))
    high_t[...] = head.astype(BF16)
    low_t[...] = tail.astype(BF16)

    def add_trail(tile, carry):
        base = pl.multiple_of(tile * TILE_A, TILE_A)
        at = onehot(base, TILE_A)
        trail[pl.ds(base, TILE_A), :] = trail[pl.ds(base, TILE_A), :] + (
            dot(at, high_t[...], NN) + dot(at, low_t[...], NN)
        )
        return carry

    tiles = total // TILE_A
    cuts = [0, 3 * tiles // 8, 6 * tiles // 8, tiles]
    tasks = [[inverse_rows[3].collect, window[1].back], [inverse_rows[3].back], []]
    for part_at in range(3):
        lax.fori_loop(cuts[part_at], cuts[part_at + 1], add_trail, 0)
        rows = pl.ds(cuts[part_at] * TILE_A, (cuts[part_at + 1] - cuts[part_at]) * TILE_A)
        outs.append(pltpu.make_async_copy(trail.at[rows, :], trail_out.at[rows, :], out_sem.at[2 + part_at]))
        outs[-1].start()
        for task in tasks[part_at]:
            task()

    for one in window:
        one.end()
    outs.append(pltpu.make_async_copy(win_full, win_out, out_sem.at[5]))
    outs[-1].start()
    for one in inverse_rows:
        one.end()
    outs.append(pltpu.make_async_copy(w_full, w_out, out_sem.at[6]))
    outs[-1].start()

    for n in range(NFRONT - 1):
        exchange(send_i, got_i, 0, n).wait_send()
        exchange(send_p, got_p, 1, n).wait_send()
        exchange(send_t, got_t, 2, n).wait_send()
    for one in window + inverse_rows:
        one.sent()
    for one in outs:
        one.wait()


def gather(front_block, blocks, rows, dest, owner):
    vmem = pl.BlockSpec(memory_space=pltpu.VMEM)
    smem = pl.BlockSpec(memory_space=pltpu.SMEM)
    hbm = pl.BlockSpec(memory_space=pl.ANY)
    dma = pltpu.SemaphoreType.DMA
    total = front_block.shape[1]
    size = WIN // HALVES

    def buf(*shape, dtype=F32):
        return pltpu.VMEM(shape, dtype)

    return pl.pallas_call(
        gather_kernel,
        out_shape=[
            jax.ShapeDtypeStruct((total, PB), F32),
            jax.ShapeDtypeStruct((total, WIN), F32),
            jax.ShapeDtypeStruct((WIN, PB), F32),
            jax.ShapeDtypeStruct((PB, PB), F32),
            jax.ShapeDtypeStruct((PB, PB), F32),
        ],
        in_specs=[hbm, vmem, vmem, smem, smem],
        out_specs=[hbm] * 5,
        scratch_shapes=[
            buf(total, PB), buf(total, WIN), buf(8, 128, dtype=jnp.int32),
            buf(NFRONT, SLOT, PB), buf(NFRONT, SLOT, WIN), buf(NFRONT, 8, 128, dtype=jnp.int32),
            buf(NFRONT, SLOT, PB), buf(NFRONT, SLOT, WIN), buf(NFRONT, 8, 128, dtype=jnp.int32),
            buf(PB, PB), buf(PB, PB), buf(NB, NB),
            buf(KALL, WIN, dtype=BF16), buf(KALL, WIN, dtype=BF16),
            buf(HALVES, size // 2, PB), buf(HALVES, size // 2, PB),
            buf(HALVES, NCHIP - 1, size // 8, PB), buf(WIN, PB),
            buf(STEPS, NB // 2, PB), buf(STEPS, NB // 2, PB),
            buf(STEPS, NCHIP - 1, NB // 8, PB), buf(PB, PB),
            dma((2,)), dma((3,)), dma((3, NFRONT)), dma((3, NFRONT)),
            dma((HALVES, 4 * NCHIP)), dma((STEPS, 4 * NCHIP)), dma((7,)),
        ],
        compiler_params=pltpu.CompilerParams(
            collective_id=0, has_side_effects=True, vmem_limit_bytes=56 * 2**20
        ),
        name="gather",
    )(front_block, blocks, rows, dest, owner)


TILE = 512


def finish_kernel(owner_ref, a_ref, b_ref, w_ref, win_ref, sym_ref, panel_ref, schur_ref, wa, wb, vv):
    step = pl.program_id(0)

    def solve(left):
        lh, ll = split(left)
        lh, ll = lh.astype(BF16), ll.astype(BF16)
        half = PB // 2
        near = jnp.concatenate([lh[:, :half], lh[:, :half], ll[:, :half]], axis=1)
        return jnp.concatenate([dot(near, wa[...], NT), dot(jnp.concatenate([lh, lh, ll], axis=1), wb[...], NT)], axis=1)

    @pl.when(step == 0)
    def _():
        high, low = split(w_ref[...])
        high, low = high.astype(BF16), low.astype(BF16)
        half = PB // 2
        wa[...] = jnp.concatenate([high[:half, :half], low[:half, :half], high[:half, :half]], axis=1)
        wb[...] = jnp.concatenate([high[half:], low[half:], high[half:]], axis=1)
        high, low = split(solve(win_ref[...]))
        high, low = high.astype(BF16), low.astype(BF16)
        vv[...] = jnp.concatenate([high, low, high], axis=1)

    solved = solve(a_ref[...])
    panel_ref[0] = solved
    sh, sl = split(solved)
    sh, sl = sh.astype(BF16), sl.astype(BF16)
    product = dot(jnp.concatenate([sh, sh, sl], axis=1), vv[...], NT)
    schur_ref[0] = b_ref[...] - product

    @pl.when((step < PB // TILE) & (owner_ref[0] == owner_ref[1]))
    def _():
        top = pl.multiple_of(step * TILE, TILE)
        factor = solve(sym_ref[pl.ds(top, TILE), :])
        row = lax.broadcasted_iota(jnp.int32, (TILE, PB), 0) + top
        panel_ref[0] = jnp.where(row >= lax.broadcasted_iota(jnp.int32, (TILE, PB), 1), factor, 0.0)


def finish(owner2, a, b, w, window, sym):
    rows = a.shape[0]
    smem = pl.BlockSpec(memory_space=pltpu.SMEM)

    def whole(v):
        return pl.BlockSpec(v.shape, lambda i: (0, 0), pipeline_mode=pl.Buffered(1))

    return pl.pallas_call(
        finish_kernel,
        grid=(rows // TILE,),
        out_shape=[jax.ShapeDtypeStruct((1, rows, PB), F32), jax.ShapeDtypeStruct((1, rows, WIN), F32)],
        in_specs=[smem, pl.BlockSpec((TILE, PB), lambda i: (i, 0)), pl.BlockSpec((TILE, WIN), lambda i: (i, 0))]
        + [whole(v) for v in (w, window, sym)],
        out_specs=[
            pl.BlockSpec((1, TILE, PB), lambda i: (0, i, 0)),
            pl.BlockSpec((1, TILE, WIN), lambda i: (0, i, 0)),
        ],
        scratch_shapes=[
            pltpu.VMEM((PB // 2, 3 * PB // 2), BF16), pltpu.VMEM((PB // 2, 3 * PB), BF16),
            pltpu.VMEM((WIN, 3 * PB), BF16),
        ],
        compiler_params=pltpu.CompilerParams(vmem_limit_bytes=56 * 2**20),
        name="finish",
    )(owner2, a, b, w, window, sym)


def local(front_block, child_blocks, child_rows, child_dest, panel_owner):
    panel, trail, window, w, sym = gather(
        front_block, child_blocks[0, 0], child_rows[0, 0], child_dest.reshape(KB), panel_owner
    )
    owner2 = jnp.concatenate([panel_owner, lax.axis_index("grp").astype(jnp.int32)[None]])
    return tuple(finish(owner2, panel, trail, w, window, sym))


def solution(mesh):
    placed = (
        P("front", "grp", None),
        P("front", "grp", None, None, None),
        P("front", "grp", None, None),
        P("front", "grp", None, None),
        P("front"),
    )
    return jax.shard_map(
        local,
        mesh=mesh,
        in_specs=placed,
        out_specs=(P("front", "grp", None), P("front", "grp", None)),
        check_vma=False,
    )
```

```python
import functools

import jax
import jax.numpy as jnp
from jax import lax
from jax.experimental import pallas as pl
from jax.experimental.pallas import tpu as pltpu
from jax.sharding import PartitionSpec as P

F32, BF16 = jnp.float32, jnp.bfloat16
MESH = pl.DeviceIdType.MESH
PB, WIN, KB, BR, CAP = 512, 896, 4, 16, 2
NFRONT, NCHIP = 16, 4
SLOT = CAP * BR
KALL = NFRONT * SLOT
NB = 128
STEPS = PB // NB
SB = 16
HALVES = 2

NN = (((1,), (0,)), ((), ()))
NT = (((1,), (1,)), ((), ()))
TN = (((0,), (0,)), ((), ()))


def split(x):
    high = x.astype(BF16).astype(F32)
    return high, x - high


def dot(a, b, dims):
    return lax.dot_general(a.astype(BF16), b.astype(BF16), dims, preferred_element_type=F32)


def dot3(a, b, dims):
    ah, al = split(a)
    bh, bl = split(b)
    return dot(ah, bh, dims) + (dot(ah, bl, dims) + dot(al, bh, dims))


def eliminate(d_ref, k):
    n, b, c0 = NB, SB, k * SB
    lane = lax.broadcasted_iota(jnp.int32, (1, n), 1)
    rows = [d_ref[pl.ds(c0 + i, 1), :] for i in range(b)]
    s = [[None] * b for _ in range(b)]
    for j in range(b):
        for i in range(j, b):
            s[i][j] = jnp.broadcast_to(rows[j][:, c0 + i : c0 + i + 1], (1, n))
    inside = (lane >= c0) & (lane < c0 + b)
    rows = [jnp.where(inside, jnp.where(lane == c0 + i, 1.0, 0.0), rows[i]) for i in range(b)]
    for j in range(b):
        inv = lax.rsqrt(s[j][j])
        for i in range(j + 1, b):
            s[i][j] = s[i][j] * inv
        rows[j] = rows[j] * inv
        for i in range(j + 1, b):
            for q in range(j + 1, i + 1):
                s[i][q] = s[i][q] - s[i][j] * s[q][j]
        for i in range(j + 1, b):
            rows[i] = rows[i] - s[i][j] * rows[j]
        d_ref[pl.ds(c0 + j, 1), :] = rows[j]
    if c0 + b < n:
        u = d_ref[pl.ds(c0, b), :]
        col = lax.broadcasted_iota(jnp.int32, (b, n), 1)
        left = jnp.where(col >= c0 + b, u, 0.0)
        uh, ul = split(u)
        lh, ll = split(left)
        update = dot(jnp.concatenate([lh, lh, ll], 0), jnp.concatenate([uh, ul, uh], 0), TN)
        below = n - c0 - b
        old = d_ref[pl.ds(c0 + b, below), :]
        col = lax.broadcasted_iota(jnp.int32, (below, n), 1)
        old = jnp.where((col >= c0) & (col < c0 + b), 0.0, old)
        d_ref[pl.ds(c0 + b, below), :] = old - update[c0 + b :, :]


HOPS = [(dx, dz) for dx in range(4) for dz in range(4)][1:]
HOPS.sort(key=lambda p: -(min(p[0], 4 - p[0]) + min(p[1], 4 - p[1])))
TILE_A = 256
FIRST, EVERY = 4, 1


class Spread:
    def __init__(self, ids, flags, src, full, base, rows, width, pre, cand, part, sems):
        self.chip, self.core, self.partner = ids
        self.own_me, self.shift = flags
        self.src, self.full, self.base, self.rows, self.width = src, full, base, rows, width
        self.pre, self.cand, self.part, self.sems = pre, cand, part, sems

    def copy(self, src, dst, sem, to):
        return pltpu.make_async_remote_copy(
            src_ref=src, dst_ref=dst, send_sem=self.sems.at[2 * sem], recv_sem=self.sems.at[2 * sem + 1],
            device_id={"grp": to}, device_id_type=MESH,
        )

    def cut(self, ref, start, size):
        return ref.at[pl.ds(start, size), pl.ds(0, self.width)]

    def other(self, step):
        return lax.rem(self.chip + step, NCHIP)

    def first(self):
        half = self.rows // 2
        return self.copy(
            self.cut(self.src[0], self.src[1] + (1 - self.core) * half, half), self.cut(self.pre, 0, half), 0, self.partner
        )

    def second(self, step):
        size = self.rows // 8
        to = self.other(step)
        return self.copy(
            self.cut(self.cand, to * size, size),
            self.part.at[step - 1, :, pl.ds(0, self.width)], step, 2 * to + self.core,
        )

    def third(self, step):
        size = self.rows // 8
        at = self.base + self.core * (self.rows // 2) + self.chip * size
        return self.copy(
            self.cut(self.full, at, size), self.cut(self.full, at, size), NCHIP - 1 + step, 2 * self.other(step) + self.core
        )

    def fourth(self):
        half = self.rows // 2
        at = self.base + self.core * half
        return self.copy(self.cut(self.full, at, half), self.cut(self.full, at, half), 2 * NCHIP - 1, self.partner)

    def pairs(self):
        self.first().start()

    def scatter(self):
        self.first().wait_recv()
        half, cols = self.rows // 2, pl.ds(0, self.width)
        own = self.src[0][pl.ds(self.src[1] + self.core * half, half), cols]
        self.cand[:, cols] = jnp.where(self.own_me, own, self.pre[:, cols])
        for step in range(1, NCHIP):
            self.second(step).start()

    def collect(self):
        size, cols = self.rows // 8, pl.ds(0, self.width)
        value = self.cand[pl.ds(self.chip * size, size), cols]
        for step in range(1, NCHIP):
            self.second(step).wait_recv()
            value = jnp.where(self.shift == step, self.part[step - 1, :, cols], value)
        self.full[pl.ds(self.base + self.core * (self.rows // 2) + self.chip * size, size), cols] = value
        for step in range(1, NCHIP):
            self.third(step).start()

    def back(self):
        for step in range(1, NCHIP):
            self.third(step).wait_recv()
        self.fourth().start()

    def end(self):
        self.fourth().wait_recv()

    def sent(self):
        self.first().wait_send()
        self.fourth().wait_send()
        for step in range(1, NCHIP):
            self.second(step).wait_send()
            self.third(step).wait_send()


def gather_kernel(
    front_ref, blocks_ref, rows_ref, dest_ref, owner_ref,
    panel_out, trail_out, win_out, w_out, sym_out,
    part, trail, rowbuf, send_p, send_t, send_i, got_p, got_t, got_i,
    table, symm, diag, high_t, low_t, win_pre, win_cand, win_part, win_full, w_pre, w_cand, w_part, w_full,
    load_sem, own_sem, xs_sem, xr_sem, win_sem, w_sem, out_sem,
):
    front = lax.axis_index("front")
    group = lax.axis_index("grp")
    chip, core = group // 2, group % 2
    x, z = front // 4, front % 4
    rest = PB + WIN
    total = front_ref.shape[1]

    loads = [
        pltpu.make_async_copy(front_ref.at[0, pl.ds(0, total), pl.ds(0, PB)], part, load_sem.at[0]),
        pltpu.make_async_copy(front_ref.at[0, pl.ds(0, total), pl.ds(PB, WIN)], trail, load_sem.at[1]),
    ]
    loads[0].start()

    barrier = pltpu.get_barrier_semaphore()

    def after_me(hop):
        return lax.rem(x + hop[0], 4) * 4 + lax.rem(z + hop[1], 4)

    def before_me(hop):
        return lax.rem(x + 4 - hop[0], 4) * 4 + lax.rem(z + 4 - hop[1], 4)

    for hop in HOPS:
        pl.semaphore_signal(barrier, inc=1, device_id={"front": after_me(hop)}, device_id_type=MESH)
    partner = 2 * chip + (1 - core)
    pl.semaphore_signal(barrier, inc=1, device_id={"grp": partner}, device_id_type=MESH)
    for step in range(1, NCHIP):
        there = 2 * lax.rem(chip + step, NCHIP) + core
        pl.semaphore_signal(barrier, inc=1, device_id={"grp": there}, device_id_type=MESH)

    rowbuf[...] = jnp.zeros_like(rowbuf)
    rowbuf[0:KB, 0:BR] = rows_ref[...]
    spread = rowbuf[...]
    for width in (16, 32, 64):
        spread = spread + pltpu.roll(spread, width, 1)
    rowbuf[...] = spread
    dests = [dest_ref[k] for k in range(KB)]
    ranks = []
    for k in range(KB):
        rank = jnp.int32(0)
        for e in range(k):
            rank = rank + (dests[e] == dests[k]).astype(jnp.int32)
        ranks.append(rank)
    lane = lax.broadcasted_iota(jnp.int32, (8, 128), 1)
    mine = lax.rem(front, 4) * SLOT

    def choose(to, slot):
        pick, found = jnp.int32(0), jnp.int32(0)
        for k in range(KB):
            hit = ((dests[k] == to) & (ranks[k] == slot)).astype(jnp.int32)
            pick = pick + hit * k
            found = found + hit
        return pick, found

    def pack_panel(to, carry):
        index = jnp.zeros((8, 128), jnp.int32)
        for slot in range(CAP):
            pick, found = choose(to, slot)
            send_p[to, slot * BR : (slot + 1) * BR, :] = blocks_ref[pick, :, 0:PB]
            at = jnp.broadcast_to(rowbuf[pl.ds(pick, 1), :], (8, 128))
            at = jnp.where(found > 0, at, -1)
            base = mine + slot * BR
            index = jnp.where((lane >= base) & (lane < base + BR), at, index)
        send_i[to] = index
        return carry

    lax.fori_loop(0, NFRONT, pack_panel, 0)
    pl.semaphore_wait(barrier, NFRONT - 1 + 1 + NCHIP - 1)

    def exchange(src, dst, kind, n):
        to = after_me(HOPS[n])
        return pltpu.make_async_remote_copy(
            src_ref=src.at[to], dst_ref=dst.at[front],
            send_sem=xs_sem.at[kind, n], recv_sem=xr_sem.at[kind, n],
            device_id={"front": to}, device_id_type=MESH,
        )

    def arrival(src, dst, kind, n):
        came = before_me(HOPS[n])
        return pltpu.make_async_remote_copy(
            src_ref=src.at[came], dst_ref=dst.at[came],
            send_sem=xs_sem.at[kind, n], recv_sem=xr_sem.at[kind, n],
            device_id={"front": came}, device_id_type=MESH,
        )

    for n in range(NFRONT - 1):
        exchange(send_i, got_i, 0, n).start()
        exchange(send_p, got_p, 1, n).start()
    owns = [
        pltpu.make_async_copy(send_i.at[front], got_i.at[front], own_sem.at[0]),
        pltpu.make_async_copy(send_p.at[front], got_p.at[front], own_sem.at[1]),
        pltpu.make_async_copy(send_t.at[front], got_t.at[front], own_sem.at[2]),
    ]
    owns[0].start()
    owns[1].start()
    loads[1].start()

    def pack_trail(to, carry):
        for slot in range(CAP):
            pick, _ = choose(to, slot)
            send_t[to, slot * BR : (slot + 1) * BR, :] = blocks_ref[pick, :, PB:]
        return carry

    lax.fori_loop(0, NFRONT, pack_trail, 0)
    owns[2].start()

    loads[0].wait()
    owns[0].wait()
    owns[1].wait()
    for n in range(NFRONT - 1):
        arrival(send_i, got_i, 0, n).wait_recv()
        arrival(send_p, got_p, 1, n).wait_recv()

    pieces = []
    for q in range(NFRONT // 4):
        piece = got_i[4 * q, 0:1, :]
        for s in range(1, 4):
            piece = piece + got_i[4 * q + s, 0:1, :]
        pieces.append(piece)
    index = jnp.concatenate(pieces, axis=1)
    high, low = split(got_p[...].reshape(KALL, PB))
    high, low = high.astype(BF16), low.astype(BF16)

    def onehot(base, size):
        at = lax.broadcasted_iota(jnp.int32, (size, KALL), 0) + base
        return jnp.where(at == index, 1.0, 0.0).astype(BF16)

    def assemble(tile, carry):
        base = pl.multiple_of(tile * TILE_A, TILE_A)
        at = onehot(base, TILE_A)
        part[pl.ds(base, TILE_A), :] = part[pl.ds(base, TILE_A), :] + (dot(at, high, NN) + dot(at, low, NN))
        return carry

    near = -(-rest // TILE_A)
    lax.fori_loop(0, near, assemble, 0)
    outs = [
        pltpu.make_async_copy(part, panel_out, out_sem.at[0]),
        pltpu.make_async_copy(symm, sym_out, out_sem.at[1]),
    ]

    owner = owner_ref[0]
    ids = (chip, core, partner)
    flags = (owner == group, lax.rem(chip - owner // 2 + NCHIP, NCHIP))
    size = WIN // HALVES
    window = [
        Spread(ids, flags, (part, PB + h * size), win_full, h * size, size, PB,
               win_pre.at[h], win_cand.at[h], win_part.at[h], win_sem.at[h])
        for h in range(HALVES)
    ]
    inverse_rows = [
        Spread(ids, flags, (table, k * NB), w_full, k * NB, NB, NB * (k + 1),
               w_pre.at[k], w_cand.at[k], w_part.at[k], w_sem.at[k])
        for k in range(STEPS)
    ]
    for one in window:
        one.pairs()

    pivot = part[0:PB, :]
    sym = 0.5 * (pivot + pivot.T)
    symm[...] = sym
    table[...] = sym
    w_full[...] = jnp.zeros_like(w_full)

    plan = {
        (0, 0): [window[0].scatter],
        (0, 2): [window[1].scatter],
        (0, 6): [outs[1].start],
        (1, 2): [window[0].collect],
        (1, 3): [inverse_rows[0].scatter],
        (2, 1): [window[1].collect],
        (2, 2): [inverse_rows[0].collect],
        (2, 3): [inverse_rows[1].scatter],
        (2, 5): [window[0].back],
        (2, 7): [inverse_rows[1].collect],
        (3, 0): [inverse_rows[0].back],
        (3, 2): [inverse_rows[2].scatter],
        (3, 4): [window[1].back],
        (3, 5): [inverse_rows[1].back],
        (3, 6): [inverse_rows[2].collect],
    }
    for n in range(NFRONT - 1):
        at = FIRST + EVERY * n
        plan.setdefault((at // (NB // SB), at % (NB // SB)), []).append(exchange(send_t, got_t, 2, n).start)

    wide = lax.broadcasted_iota(jnp.int32, (NB, PB), 1)
    for k in range(STEPS):
        base = k * NB
        diag[...] = table[base : base + NB, base : base + NB]
        for ib in range(NB // SB):
            eliminate(diag, ib)
            for task in plan.get((k, ib), ()):
                task()
        inverse = jnp.where(
            lax.broadcasted_iota(jnp.int32, (NB, NB), 0) >= lax.broadcasted_iota(jnp.int32, (NB, NB), 1),
            diag[...], 0.0,
        )
        above = table[base : base + NB, :]
        above = jnp.where((wide >= base) & (wide < base + NB), 0.0, above)
        reduced = dot3(inverse, above, NN)
        table[base : base + NB, :] = reduced
        table[base : base + NB, base : base + NB] = inverse
        inverse_rows[k].pairs()
        if k + 1 < STEPS:
            upper = table[base : base + NB, :]
            left = reduced[:, base + NB :]
            update = dot3(left, upper, TN)
            old = table[base + NB :, :]
            col = lax.broadcasted_iota(jnp.int32, old.shape, 1)
            old = jnp.where((col >= base) & (col < base + NB), 0.0, old)
            table[base + NB :, :] = old - update

    inverse_rows[3].scatter()
    inverse_rows[2].back()
    lax.fori_loop(near, total // TILE_A, assemble, 0)
    outs[0].start()

    loads[1].wait()
    owns[2].wait()
    for n in range(NFRONT - 1):
        arrival(send_t, got_t, 2, n).wait_recv()
    head, tail = split(got_t[...].reshape(KALL, WIN))
    high_t[...] = head.astype(BF16)
    low_t[...] = tail.astype(BF16)

    def add_trail(tile, carry):
        base = pl.multiple_of(tile * TILE_A, TILE_A)
        at = onehot(base, TILE_A)
        trail[pl.ds(base, TILE_A), :] = trail[pl.ds(base, TILE_A), :] + (
            dot(at, high_t[...], NN) + dot(at, low_t[...], NN)
        )
        return carry

    tiles = total // TILE_A
    cuts = [0, 3 * tiles // 8, 6 * tiles // 8, tiles]
    tasks = [[inverse_rows[3].collect], [inverse_rows[3].back], []]
    for part_at in range(3):
        lax.fori_loop(cuts[part_at], cuts[part_at + 1], add_trail, 0)
        rows = pl.ds(cuts[part_at] * TILE_A, (cuts[part_at + 1] - cuts[part_at]) * TILE_A)
        outs.append(pltpu.make_async_copy(trail.at[rows, :], trail_out.at[rows, :], out_sem.at[2 + part_at]))
        outs[-1].start()
        for task in tasks[part_at]:
            task()

    for one in window:
        one.end()
    outs.append(pltpu.make_async_copy(win_full, win_out, out_sem.at[5]))
    outs[-1].start()
    for one in inverse_rows:
        one.end()
    outs.append(pltpu.make_async_copy(w_full, w_out, out_sem.at[6]))
    outs[-1].start()

    for n in range(NFRONT - 1):
        exchange(send_i, got_i, 0, n).wait_send()
        exchange(send_p, got_p, 1, n).wait_send()
        exchange(send_t, got_t, 2, n).wait_send()
    for one in window + inverse_rows:
        one.sent()
    for one in outs:
        one.wait()


def gather(front_block, blocks, rows, dest, owner):
    vmem = pl.BlockSpec(memory_space=pltpu.VMEM)
    smem = pl.BlockSpec(memory_space=pltpu.SMEM)
    hbm = pl.BlockSpec(memory_space=pl.ANY)
    dma = pltpu.SemaphoreType.DMA
    total = front_block.shape[1]
    size = WIN // HALVES

    def buf(*shape, dtype=F32):
        return pltpu.VMEM(shape, dtype)

    return pl.pallas_call(
        gather_kernel,
        out_shape=[
            jax.ShapeDtypeStruct((total, PB), F32),
            jax.ShapeDtypeStruct((total, WIN), F32),
            jax.ShapeDtypeStruct((WIN, PB), F32),
            jax.ShapeDtypeStruct((PB, PB), F32),
            jax.ShapeDtypeStruct((PB, PB), F32),
        ],
        in_specs=[hbm, vmem, vmem, smem, smem],
        out_specs=[hbm] * 5,
        scratch_shapes=[
            buf(total, PB), buf(total, WIN), buf(8, 128, dtype=jnp.int32),
            buf(NFRONT, SLOT, PB), buf(NFRONT, SLOT, WIN), buf(NFRONT, 8, 128, dtype=jnp.int32),
            buf(NFRONT, SLOT, PB), buf(NFRONT, SLOT, WIN), buf(NFRONT, 8, 128, dtype=jnp.int32),
            buf(PB, PB), buf(PB, PB), buf(NB, NB),
            buf(KALL, WIN, dtype=BF16), buf(KALL, WIN, dtype=BF16),
            buf(HALVES, size // 2, PB), buf(HALVES, size // 2, PB),
            buf(HALVES, NCHIP - 1, size // 8, PB), buf(WIN, PB),
            buf(STEPS, NB // 2, PB), buf(STEPS, NB // 2, PB),
            buf(STEPS, NCHIP - 1, NB // 8, PB), buf(PB, PB),
            dma((2,)), dma((3,)), dma((3, NFRONT)), dma((3, NFRONT)),
            dma((HALVES, 4 * NCHIP)), dma((STEPS, 4 * NCHIP)), dma((7,)),
        ],
        compiler_params=pltpu.CompilerParams(
            collective_id=0, has_side_effects=True, vmem_limit_bytes=56 * 2**20
        ),
        name="gather",
    )(front_block, blocks, rows, dest, owner)


TILE = 512


def finish_kernel(owner_ref, a_ref, b_ref, w_ref, win_ref, sym_ref, panel_ref, schur_ref, wa, wb, vv):
    step = pl.program_id(0)

    def solve(left):
        lh, ll = split(left)
        lh, ll = lh.astype(BF16), ll.astype(BF16)
        half = PB // 2
        near = jnp.concatenate([lh[:, :half], lh[:, :half], ll[:, :half]], axis=1)
        return jnp.concatenate([dot(near, wa[...], NT), dot(jnp.concatenate([lh, lh, ll], axis=1), wb[...], NT)], axis=1)

    @pl.when(step == 0)
    def _():
        high, low = split(w_ref[...])
        high, low = high.astype(BF16), low.astype(BF16)
        half = PB // 2
        wa[...] = jnp.concatenate([high[:half, :half], low[:half, :half], high[:half, :half]], axis=1)
        wb[...] = jnp.concatenate([high[half:], low[half:], high[half:]], axis=1)
        high, low = split(solve(win_ref[...]))
        high, low = high.astype(BF16), low.astype(BF16)
        vv[...] = jnp.concatenate([high, low, high], axis=1)

    solved = solve(a_ref[...])
    panel_ref[0] = solved
    sh, sl = split(solved)
    sh, sl = sh.astype(BF16), sl.astype(BF16)
    product = dot(jnp.concatenate([sh, sh, sl], axis=1), vv[...], NT)
    schur_ref[0] = b_ref[...] - product

    @pl.when((step < PB // TILE) & (owner_ref[0] == lax.axis_index("grp")))
    def _():
        top = pl.multiple_of(step * TILE, TILE)
        factor = solve(sym_ref[pl.ds(top, TILE), :])
        row = lax.broadcasted_iota(jnp.int32, (TILE, PB), 0) + top
        panel_ref[0] = jnp.where(row >= lax.broadcasted_iota(jnp.int32, (TILE, PB), 1), factor, 0.0)


def finish(owner, a, b, w, window, sym):
    rows = a.shape[0]
    smem = pl.BlockSpec(memory_space=pltpu.SMEM)

    def whole(v):
        return pl.BlockSpec(v.shape, lambda i: (0, 0), pipeline_mode=pl.Buffered(1))

    return pl.pallas_call(
        finish_kernel,
        grid=(rows // TILE,),
        out_shape=[jax.ShapeDtypeStruct((1, rows, PB), F32), jax.ShapeDtypeStruct((1, rows, WIN), F32)],
        in_specs=[smem, pl.BlockSpec((TILE, PB), lambda i: (i, 0)), pl.BlockSpec((TILE, WIN), lambda i: (i, 0))]
        + [whole(v) for v in (w, window, sym)],
        out_specs=[
            pl.BlockSpec((1, TILE, PB), lambda i: (0, i, 0)),
            pl.BlockSpec((1, TILE, WIN), lambda i: (0, i, 0)),
        ],
        scratch_shapes=[
            pltpu.VMEM((PB // 2, 3 * PB // 2), BF16), pltpu.VMEM((PB // 2, 3 * PB), BF16),
            pltpu.VMEM((WIN, 3 * PB), BF16),
        ],
        compiler_params=pltpu.CompilerParams(vmem_limit_bytes=56 * 2**20),
        name="finish",
    )(owner, a, b, w, window, sym)


def local(front_block, child_blocks, child_rows, child_dest, panel_owner):
    panel, trail, window, w, sym = gather(
        front_block, child_blocks[0, 0], child_rows[0, 0], child_dest.reshape(KB), panel_owner
    )
    return tuple(finish(panel_owner, panel, trail, w, window, sym))


def solution(mesh):
    placed = (
        P("front", "grp", None),
        P("front", "grp", None, None, None),
        P("front", "grp", None, None),
        P("front", "grp", None, None),
        P("front"),
    )
    return jax.shard_map(
        local,
        mesh=mesh,
        in_specs=placed,
        out_specs=(P("front", "grp", None), P("front", "grp", None)),
        check_vma=False,
    )
```
